32 devices in a mesh: tok: 8 (over z, y), head: 4 (over x, core).
Axes of the slice: x: 2, y: 2, z: 4, core: 2. Of those that a mesh axis runs over, the one named last changes fastest.
Arguments:
- query: bfloat16 [1024, 8192], P('tok', 'head'), may hold values from -5 to 5
- keys: bfloat16 [1024, 1024], P(('tok', 'head')), may hold values from -5 to 5
- values: bfloat16 [1024, 1024], P(('tok', 'head')), may hold values from -6 to 6
- out_grad: bfloat16 [1024, 8192], P('tok', 'head'), may hold values from -6 to 6
- log_norm: float32 [64, 1024], P('head', 'tok'), may hold values from 4 to 6
- row_dot: float32 [64, 1024], P('head', 'tok'), may hold values from -24 to 24
- doc_start: int32 [1024], replicated, may hold values from 0 to 1023, as said below
- spans: int32 [8], replicated, may hold values from 1 to 6, as said below
Outputs:
- query_grad: bfloat16 [1024, 8192], P('tok', 'head')
- key_grad: bfloat16 [1024, 1024], P('tok', 'head')
- value_grad: bfloat16 [1024, 1024], P('tok', 'head')
The draws below stay inside these ranges and needn't reach their ends.
Inputs may be any that keep to these rules, and one draw needn't show every extreme that they name: doc_start[t] <= t, doc_start[0] = 0, doc_start never falls along t, and doc_start[t] = t where a document begins; the last position always begins a document of one token. Query block g (tokens g * 128 to g * 128 + 127) reads the spans[g] key blocks that end with block g itself. In every draw at least one query block has span 6.
All inputs are finite; a program needn't handle non-finite values.
Results may differ from the reference program's by a relative error of at most 0.008.
Values may be sent and summed in bfloat16 or wider, within the bound.
No kernel may reach another device: no remote copies, remote signals or barrier semaphores. Data moves between devices by JAX's collectives and lax.ppermute only.
A program may use at most 64 MiB of HBM per device.

```python
import math
import jax
import jax.numpy as jnp
from jax import lax

HEADS = 64
KV_HEADS = 8
HEAD_DIM = 128
QBLOCK = 128
SPAN_MAX = 6
QB_DEV = 1
TOKENS = 1024
QBLOCKS = 8


def scaled_rows(key, rows, columns):
    return jnp.clip(jax.random.normal(key, (rows, columns), jnp.float32), -5.0, 5.0)


def draw_query(key, part):
    return scaled_rows(jax.random.fold_in(key, 11), TOKENS, HEADS * HEAD_DIM).astype(jnp.bfloat16)


def draw_keys(key, part):
    return scaled_rows(jax.random.fold_in(key, 23), TOKENS, KV_HEADS * HEAD_DIM).astype(jnp.bfloat16)


def draw_doc_start(key, part):
    positions = jnp.arange(TOKENS, dtype=jnp.int32)
    marks = jax.random.randint(jax.random.fold_in(key, 31), (TOKENS,), 0, 8 * QBLOCK) == 0
    marks = marks | (positions == TOKENS - 1)
    begins = jnp.where(marks, positions, 0).astype(jnp.int32)
    return lax.cummax(begins, axis=0).astype(jnp.int32)


def draw_spans(key, part):
    groups = QBLOCKS // QB_DEV
    base_key = jax.random.fold_in(key, 47)
    first_key, second_key, third_key = jax.random.split(base_key, 3)
    heavy = jax.random.randint(first_key, (groups,), 0, 16) == 0
    chosen = jax.random.randint(third_key, (), 0, groups)
    heavy = heavy | (jnp.arange(groups, dtype=jnp.int32) == chosen)
    light = jax.random.randint(second_key, (groups, QB_DEV), 1, 4)
    spread = jnp.where(heavy[:, None], SPAN_MAX, light)
    return spread.reshape(QBLOCKS).astype(jnp.int32)


def shard_levels(stream_key, extent, cuts, least, high):
    def one(position, blocks):
        heights = jax.random.uniform(jax.random.fold_in(jax.random.fold_in(stream_key, 6), position), (blocks,), jnp.float32, least / len(cuts), high / len(cuts))
        return jnp.repeat(jnp.exp(heights), extent[position] // blocks).reshape((-1,) + (1,) * (len(extent) - position - 1))

    factor_of = one(*cuts[0])
    for cut in cuts[1:]:
        factor_of = factor_of * one(*cut)
    return factor_of


def gaussian(rng, shape, scale, reach, cuts=(), held_as=jnp.bfloat16):
    array = jax.random.normal(rng, shape, jnp.float32) * scale
    if len(cuts) > 0:
        array = shard_levels(rng, shape, cuts, -0.22, 0.18) * array
    return jnp.clip(array, min=-reach, max=reach).astype(held_as)


def setup_inputs(seed: int = 0) -> dict:
    seeds = jax.random.split(jax.random.key(seed), 9)
    return {
        "query": draw_query(jax.random.fold_in(seeds[8], 71), 0),
        "keys": draw_keys(jax.random.fold_in(seeds[8], 71), 0),
        "values": gaussian(seeds[2], (TOKENS, KV_HEADS * HEAD_DIM), 1.0, 6.0, ((0, 32),)),
        "out_grad": gaussian(seeds[3], (TOKENS, HEADS * HEAD_DIM), 1.0, 6.0, ((0, 8), (1, 4))),
        "log_norm": jnp.clip(4.0 + 2.0 * jax.random.uniform(seeds[4], (HEADS, TOKENS), jnp.float32) ** shard_levels(seeds[4], (HEADS, TOKENS), ((0, 4), (1, 8)), -0.2, 0.2), 4.0, 6.0),
        "row_dot": gaussian(seeds[5], (HEADS, TOKENS), 4.0, 24.0, ((0, 4), (1, 8)), jnp.float32),
        "doc_start": draw_doc_start(jax.random.fold_in(seeds[8], 71), 0),
        "spans": draw_spans(jax.random.fold_in(seeds[8], 71), 0),
    }


def reference(query, keys, values, out_grad, log_norm, row_dot, doc_start, spans):
    group_size = HEADS // KV_HEADS
    head_scale = 1.0 / math.sqrt(HEAD_DIM)
    pad_rows = (SPAN_MAX - 1) * QBLOCK
    window_rows = SPAN_MAX * QBLOCK
    filler = jnp.zeros((pad_rows, KV_HEADS * HEAD_DIM), keys.dtype)
    key_wide = jnp.concatenate([filler, keys], axis=0).reshape(-1, KV_HEADS, HEAD_DIM)
    value_wide = jnp.concatenate([filler, values], axis=0).reshape(-1, KV_HEADS, HEAD_DIM)
    query_blocks = query.reshape(QBLOCKS, QBLOCK, KV_HEADS, group_size, HEAD_DIM)
    outgrad_blocks = out_grad.reshape(QBLOCKS, QBLOCK, KV_HEADS, group_size, HEAD_DIM)
    norm_blocks = log_norm.reshape(KV_HEADS, group_size, QBLOCKS, QBLOCK).transpose(2, 0, 1, 3)
    dot_blocks = row_dot.reshape(KV_HEADS, group_size, QBLOCKS, QBLOCK).transpose(2, 0, 1, 3)
    start_blocks = doc_start.reshape(QBLOCKS, QBLOCK)
    row_index = jnp.arange(QBLOCK, dtype=jnp.int32)
    window_index = jnp.arange(window_rows, dtype=jnp.int32)

    def one_block(totals, inputs):
        key_total, value_total = totals
        block_index, query_block, outgrad_block, norm_block, dot_block, start_block, span_count = inputs
        anchor = (block_index * QBLOCK).astype(jnp.int32)
        key_window = lax.dynamic_slice_in_dim(key_wide, anchor, window_rows, 0).astype(jnp.float32)
        value_window = lax.dynamic_slice_in_dim(value_wide, anchor, window_rows, 0).astype(jnp.float32)
        query_pos = anchor + row_index
        key_pos = anchor - pad_rows + window_index
        key_blockid = block_index - (SPAN_MAX - 1) + window_index // QBLOCK
        allowed = (key_pos[None, :] <= query_pos[:, None]) & (key_pos[None, :] >= start_block[:, None])
        allowed = allowed & (key_blockid[None, :] > block_index - span_count)
        query_wide = query_block.astype(jnp.float32)
        outgrad_wide = outgrad_block.astype(jnp.float32)
        scores = jnp.einsum('qagd,kad->agqk', query_wide, key_window) * head_scale
        probs = jnp.where(allowed[None, None], jnp.exp(scores - norm_block[..., None]), 0.0)
        probs_low = lax.optimization_barrier(probs.astype(jnp.bfloat16)).astype(jnp.float32)
        value_term = jnp.einsum('agqk,qagd->kad', probs_low, outgrad_wide)
        prob_grad = jnp.einsum('qagd,kad->agqk', outgrad_wide, value_window)
        score_grad = (probs * (prob_grad - dot_block[..., None])).astype(jnp.bfloat16)
        score_grad = lax.optimization_barrier(score_grad).astype(jnp.float32)
        query_term = jnp.einsum('agqk,kad->qagd', score_grad, key_window) * head_scale
        key_term = jnp.einsum('agqk,qagd->kad', score_grad, query_wide) * head_scale
        key_old = lax.dynamic_slice_in_dim(key_total, anchor, window_rows, 0)
        key_total = lax.dynamic_update_slice_in_dim(key_total, key_old + key_term, anchor, 0)
        value_old = lax.dynamic_slice_in_dim(value_total, anchor, window_rows, 0)
        value_total = lax.dynamic_update_slice_in_dim(value_total, value_old + value_term, anchor, 0)
        return ((key_total, value_total), query_term)
    zero_total = jnp.zeros((pad_rows + TOKENS, KV_HEADS, HEAD_DIM), jnp.float32)
    block_ids = jnp.arange(QBLOCKS, dtype=jnp.int32)
    finals, query_terms = lax.scan(one_block, (zero_total, zero_total), (block_ids, query_blocks, outgrad_blocks, norm_blocks, dot_blocks, start_blocks, spans))
    key_total, value_total = finals
    query_grad = query_terms.reshape(TOKENS, HEADS * HEAD_DIM).astype(jnp.bfloat16)
    key_grad = key_total[pad_rows:].reshape(TOKENS, KV_HEADS * HEAD_DIM).astype(jnp.bfloat16)
    value_grad = value_total[pad_rows:].reshape(TOKENS, KV_HEADS * HEAD_DIM).astype(jnp.bfloat16)
    return (query_grad, key_grad, value_grad)
```

```python
import functools
import math

import jax
import jax.numpy as jnp
from jax import lax
from jax.experimental import pallas as pl
from jax.experimental.pallas import tpu as pltpu
from jax.sharding import PartitionSpec as P

HEADS = 64
KV_HEADS = 8
HEAD_DIM = 128
QBLOCK = 128
REACH = 5
NEAR = 2
CASES_MAX = 16
NT = (((1,), (1,)), ((), ()))
NN = (((1,), (0,)), ((), ()))
VMEM = pl.BlockSpec(memory_space=pltpu.VMEM)
SMEM = pl.BlockSpec(memory_space=pltpu.SMEM)
PARAMS = pltpu.CompilerParams(vmem_limit_bytes=32 * 1024 * 1024)


def matmul(left, right, dims):
    return lax.dot_general(left, right, dims, preferred_element_type=jnp.float32)


def shifted(value, steps, targets=None):
    count = lax.axis_size("tok")
    if targets is None:
        targets = range(max(0, steps), min(count, count + steps))
    return lax.ppermute(value, "tok", [(target - steps, target) for target in targets])


def far_cases(toks):
    return list(range(NEAR + 1, toks)) if toks <= CASES_MAX else []


def blocks_read(tok, spans, starts):
    lowest = starts[tok * QBLOCK] // QBLOCK
    return jnp.minimum(spans[tok], tok - lowest + 1)


def pack_kernel(spans, starts, keys, values, shares, case):
    toks = spans.shape[0]
    heads, key_cols = shares.shape[0], shares.shape[-1]
    for head in range(heads):
        shares[head, 0] = keys[:, head * key_cols : (head + 1) * key_cols]
        shares[head, 1] = values[:, head * key_cols : (head + 1) * key_cols]

    def count(tok, seen):
        far = (blocks_read(tok, spans, starts) > NEAR + 1).astype(jnp.int32)
        return seen[0] + far, seen[1] + far * tok

    total, where = lax.fori_loop(0, toks, count, (jnp.int32(0), jnp.int32(0)))
    singles = len(far_cases(toks))
    several = jnp.int32(singles + 1)
    if singles:
        several = jnp.where(total == 1, where - NEAR, several)
    case[0] = jnp.where(total == 0, 0, several)


def pack(spans, doc_start, keys, values, heads):
    rows, key_cols = keys.shape[0], keys.shape[1] // heads
    return pl.pallas_call(
        pack_kernel,
        out_shape=(
            jax.ShapeDtypeStruct((heads, 2, rows, key_cols), keys.dtype),
            jax.ShapeDtypeStruct((1,), jnp.int32),
        ),
        in_specs=[SMEM, SMEM, VMEM, VMEM],
        out_specs=(VMEM, SMEM),
        name="pack_shares",
    )(spans, doc_start, keys, values)


def columns(head):
    return pl.ds(head * HEAD_DIM, HEAD_DIM)


def two(ref, head):
    return jnp.concatenate([ref[:, columns(head)], ref[:, columns(head + 1)]], axis=0)


def two_lanes(ref, head):
    return jnp.concatenate([ref[head : head + 1, :], ref[head + 1 : head + 2, :]], axis=1)


def one_block(tok, offset, slot, data, window, query_acc, store):
    query, outgrad, norm, dot, starts_rows = data
    kv_local = window.shape[-1] // HEAD_DIM
    group = query.shape[1] // HEAD_DIM // kv_local
    pairs = group // 2
    head_scale = 1.0 / math.sqrt(HEAD_DIM)
    key_row = lax.broadcasted_iota(jnp.int32, (QBLOCK, QBLOCK), 0)
    query_col = lax.broadcasted_iota(jnp.int32, (QBLOCK, QBLOCK), 1)
    key_pos = (tok - offset) * QBLOCK + key_row
    allowed = (key_pos >= starts_rows[pl.ds(tok, 1), :]) & (key_pos <= tok * QBLOCK + query_col)
    allowed = jnp.concatenate([allowed, allowed], axis=1)
    for part in range(kv_local):
        keys, values = (
            jnp.concatenate(
                [window[slot, share, which, :, columns(part)] for share in range(window.shape[1])],
                axis=0,
            )
            for which in range(2)
        )
        keys_turned = keys.T
        key_term = jnp.zeros((QBLOCK, HEAD_DIM), jnp.float32)
        value_term = jnp.zeros((QBLOCK, HEAD_DIM), jnp.float32)
        for pair in range(pairs):
            head = part * group + 2 * pair
            queries = two(query, head)
            outgrads = two(outgrad, head)
            scores = matmul(keys, queries, NT) * head_scale
            probs = jnp.where(allowed, jnp.exp(scores - two_lanes(norm, head)), 0.0)
            value_term += matmul(probs.astype(jnp.bfloat16), outgrads, NN)
            prob_grad = matmul(values, outgrads, NT)
            score_grad = (probs * (prob_grad - two_lanes(dot, head))).astype(jnp.bfloat16)
            key_term += matmul(score_grad, queries, NN)
            query_acc[part * pairs + pair] += matmul(keys_turned, score_grad, NN)
        store(part, key_term * head_scale, value_term)


def near_kernel(spans, starts, *refs):
    data, blocks = refs[:5], refs[5 : 6 + NEAR]
    own_terms, near_terms, query_acc, window = refs[6 + NEAR :]
    tok = lax.axis_index("tok")
    items = jnp.minimum(blocks_read(tok, spans, starts), NEAR + 1)
    query_acc[...] = jnp.zeros(query_acc.shape, query_acc.dtype)
    near_terms[...] = jnp.zeros(near_terms.shape, near_terms.dtype)
    for slot, block in enumerate(blocks):
        window[slot] = block[...]

    @pl.loop(0, items)
    def _(offset):
        def store(part, key_term, value_term):
            @pl.when(offset == 0)
            def _():
                own_terms[0, :, columns(part)] = key_term
                own_terms[1, :, columns(part)] = value_term

            @pl.when(offset > 0)
            def _():
                near_terms[offset - 1, 0, :, columns(part)] = key_term.astype(near_terms.dtype)
                near_terms[offset - 1, 1, :, columns(part)] = value_term.astype(near_terms.dtype)

        one_block(tok, offset, offset, data, window, query_acc, store)


def far_kernel(spans, starts, *refs):
    data, acc_in, blocks = refs[:5], refs[5], refs[6 : 6 + REACH - NEAR]
    query_grad, far_terms, query_acc, window = refs[6 + REACH - NEAR :]
    tok = lax.axis_index("tok")
    items = blocks_read(tok, spans, starts)
    head_scale = 1.0 / math.sqrt(HEAD_DIM)
    far_terms[...] = jnp.zeros(far_terms.shape, far_terms.dtype)

    def write(acc):
        for pair in range(acc.shape[0]):
            total = (acc[pair] * head_scale).astype(query_grad.dtype)
            query_grad[:, columns(2 * pair)] = total[:, :QBLOCK].T
            query_grad[:, columns(2 * pair + 1)] = total[:, QBLOCK:].T

    query_acc[...] = acc_in[...]

    @pl.when(items > NEAR + 1)
    def _():
        for slot, block in enumerate(blocks):
            window[slot] = block[...]

    @pl.loop(NEAR + 1, items)
    def _(offset):
        slot = offset - NEAR - 1

        def store(part, key_term, value_term):
            far_terms[slot, 0, :, columns(part)] = key_term.astype(far_terms.dtype)
            far_terms[slot, 1, :, columns(part)] = value_term.astype(far_terms.dtype)

        one_block(tok, offset, slot, data, window, query_acc, store)

    write(query_acc)


def sum_kernel(own, near, *refs):
    arrived, (key_grad, value_grad) = refs[:-2], refs[-2:]
    for which, out in enumerate((key_grad, value_grad)):
        total = own[which] + near[which].astype(jnp.float32)
        for term in arrived:
            total = total + term[which].astype(jnp.float32)
        out[...] = total.astype(out.dtype)


def per_device(query, keys, values, out_grad, log_norm, row_dot, doc_start, spans):
    toks, heads = lax.axis_size("tok"), lax.axis_size("head")
    key_cols = keys.shape[1] // heads
    head_pairs = query.shape[1] // (2 * HEAD_DIM)
    acc_shape = (head_pairs, HEAD_DIM, 2 * QBLOCK)
    terms = (2, QBLOCK, key_cols)
    data = (query, out_grad, log_norm, row_dot, doc_start.reshape(-1, QBLOCK))
    shares, case = pack(spans, doc_start, keys, values, heads)
    case = case[0]
    own = lax.all_to_all(shares, "head", split_axis=0, concat_axis=0)
    near = [shifted(own, steps) for steps in range(1, NEAR + 1)]
    far_steps = range(NEAR + 1, REACH + 1)

    def near_part(blocks):
        return pl.pallas_call(
            near_kernel,
            out_shape=(
                jax.ShapeDtypeStruct(terms, jnp.float32),
                jax.ShapeDtypeStruct((NEAR, *terms), jnp.bfloat16),
                jax.ShapeDtypeStruct(acc_shape, jnp.float32),
            ),
            in_specs=[SMEM, SMEM] + [VMEM] * (6 + NEAR),
            out_specs=(VMEM,) * 3,
            scratch_shapes=[pltpu.VMEM((NEAR + 1, *own.shape), own.dtype)],
            compiler_params=PARAMS,
            cost_estimate=pl.CostEstimate(
                flops=3 * 10 * QBLOCK * QBLOCK * query.shape[1],
                bytes_accessed=4 * 1024 * 1024,
                transcendentals=3 * QBLOCK * query.shape[1],
            ),
            name="near_grads",
        )(spans, doc_start, *data, *blocks)

    def fetch(targets_of):
        def run(own, near):
            far = []
            for steps in far_steps:
                targets = targets_of(steps)
                far.append(shifted(own, steps, targets) if targets else jnp.zeros_like(own))
            return (*far, *near_part((own, *near)))

        return run

    def give(targets_of):
        def run(far_terms):
            back = []
            for place, steps in enumerate(far_steps):
                targets = targets_of(steps)
                term = far_terms[place]
                if targets:
                    term = shifted(term, -steps, [target - steps for target in targets])
                else:
                    term = jnp.zeros_like(term)
                back.append(term)
            return tuple(back)

        return run

    wanted = [lambda steps: []]
    for tok in far_cases(toks):
        wanted.append(lambda steps, tok=tok: [tok] if tok >= steps else [])
    wanted.append(lambda steps: list(range(steps, toks)))
    *far, own_terms, near_terms, query_acc = lax.switch(
        case, [fetch(targets_of) for targets_of in wanted], own, near
    )
    near_back = [shifted(near_terms[steps - 1], -steps) for steps in range(1, NEAR + 1)]
    query_grad, far_terms = pl.pallas_call(
        far_kernel,
        out_shape=(
            jax.ShapeDtypeStruct(query.shape, jnp.bfloat16),
            jax.ShapeDtypeStruct((REACH - NEAR, *terms), jnp.bfloat16),
        ),
        in_specs=[SMEM, SMEM] + [VMEM] * (6 + REACH - NEAR),
        out_specs=(VMEM,) * 2,
        scratch_shapes=[
            pltpu.VMEM(acc_shape, jnp.float32),
            pltpu.VMEM((REACH - NEAR, *own.shape), own.dtype),
        ],
        compiler_params=PARAMS,
        name="far_grads",
    )(spans, doc_start, *data, query_acc, *far)
    far_back = lax.switch(case, [give(targets_of) for targets_of in wanted], far_terms)
    key_grad, value_grad = pl.pallas_call(
        sum_kernel,
        out_shape=(jax.ShapeDtypeStruct(terms[1:], jnp.bfloat16),) * 2,
        in_specs=[VMEM] * (1 + REACH),
        out_specs=(VMEM,) * 2,
        name="sum_terms",
    )(own_terms, *near_back, *far_back)
    return (query_grad, key_grad, value_grad)


def solution(mesh):
    in_specs = (
        P("tok", "head"),
        P(("tok", "head"), None),
        P(("tok", "head"), None),
        P("tok", "head"),
        P("head", "tok"),
        P("head", "tok"),
        P(),
        P(),
    )
    out_specs = (P("tok", "head"), P("tok", "head"), P("tok", "head"))
    return jax.shard_map(
        per_device, mesh=mesh, in_specs=in_specs, out_specs=out_specs, check_vma=False
    )
```

```python
import functools
import math

import jax
import jax.numpy as jnp
from jax import lax
from jax.experimental import pallas as pl
from jax.experimental.pallas import tpu as pltpu
from jax.sharding import PartitionSpec as P

HEADS = 64
KV_HEADS = 8
HEAD_DIM = 128
QBLOCK = 128
REACH = 5
NEAR = 2
CASES_MAX = 16
NT = (((1,), (1,)), ((), ()))
NN = (((1,), (0,)), ((), ()))
VMEM = pl.BlockSpec(memory_space=pltpu.VMEM)
SMEM = pl.BlockSpec(memory_space=pltpu.SMEM)
LARGE = pltpu.CompilerParams(vmem_limit_bytes=24 * 1024 * 1024)
SMALL = pltpu.CompilerParams(vmem_limit_bytes=6 * 1024 * 1024)


def matmul(left, right, dims):
    return lax.dot_general(left, right, dims, preferred_element_type=jnp.float32)


def shifted(value, steps, targets=None):
    count = lax.axis_size("tok")
    if targets is None:
        targets = range(max(0, steps), min(count, count + steps))
    return lax.ppermute(value, "tok", [(target - steps, target) for target in targets])


def far_cases(toks):
    return list(range(NEAR + 1, toks)) if toks <= CASES_MAX else []


def blocks_read(tok, spans, starts):
    lowest = starts[tok * QBLOCK] // QBLOCK
    return jnp.minimum(spans[tok], tok - lowest + 1)


def pack_kernel(spans, starts, keys, values, shares, case):
    toks = spans.shape[0]
    heads, key_cols = shares.shape[0], shares.shape[-1]
    for head in range(heads):
        shares[head, 0] = keys[:, head * key_cols : (head + 1) * key_cols]
        shares[head, 1] = values[:, head * key_cols : (head + 1) * key_cols]

    def count(tok, seen):
        far = (blocks_read(tok, spans, starts) > NEAR + 1).astype(jnp.int32)
        return seen[0] + far, seen[1] + far * tok

    total, where = lax.fori_loop(0, toks, count, (jnp.int32(0), jnp.int32(0)))
    singles = len(far_cases(toks))
    several = jnp.int32(singles + 1)
    if singles:
        several = jnp.where(total == 1, where - NEAR, several)
    case[0] = jnp.where(total == 0, 0, several)


def pack(spans, doc_start, keys, values, heads):
    rows, key_cols = keys.shape[0], keys.shape[1] // heads
    return pl.pallas_call(
        pack_kernel,
        out_shape=(
            jax.ShapeDtypeStruct((heads, 2, rows, key_cols), keys.dtype),
            jax.ShapeDtypeStruct((1,), jnp.int32),
        ),
        in_specs=[SMEM, SMEM, VMEM, VMEM],
        out_specs=(VMEM, SMEM),
        compiler_params=SMALL,
        name="pack_shares",
    )(spans, doc_start, keys, values)


def columns(head):
    return pl.ds(pl.multiple_of(head * HEAD_DIM, HEAD_DIM), HEAD_DIM)


def block_terms(tok, offset, part, block, data, store):
    queries, outgrads, norm, dot, starts_rows = data
    head_scale = 1.0 / math.sqrt(HEAD_DIM)
    heads = queries.shape[1] // QBLOCK
    key_row = lax.broadcasted_iota(jnp.int32, (QBLOCK, QBLOCK), 0)
    query_col = lax.broadcasted_iota(jnp.int32, (QBLOCK, QBLOCK), 1)
    key_pos = (tok - offset) * QBLOCK + key_row
    allowed = (key_pos >= starts_rows[pl.ds(tok, 1), :]) & (key_pos <= tok * QBLOCK + query_col)
    allowed = jnp.concatenate([allowed] * heads, axis=1)
    keys, values = (
        jnp.concatenate(
            [block[share, which, :, columns(part)] for share in range(block.shape[0])], axis=0
        )
        for which in range(2)
    )
    scores = matmul(keys, queries[part], NT) * head_scale
    probs = jnp.where(allowed, jnp.exp(scores - norm[part]), 0.0)
    value_term = matmul(probs.astype(jnp.bfloat16), outgrads[part], NN)
    prob_grad = matmul(values, outgrads[part], NT)
    score_grad = (probs * (prob_grad - dot[part])).astype(jnp.bfloat16)
    key_term = matmul(score_grad, queries[part], NN)
    query_term = matmul(keys.T, score_grad, NN)
    store(key_term * head_scale, value_term, query_term)


def own_kernel(
    query, outgrad, norm, dot, starts_rows, block, own_terms, query_acc, queries, outgrads, norms, dots
):
    tok = lax.axis_index("tok")
    parts, rows = queries.shape[:2]
    group = rows // QBLOCK
    for part in range(parts):
        for member in range(group):
            head = part * group + member
            place = slice(member * QBLOCK, (member + 1) * QBLOCK)
            queries[part, place, :] = query[:, head * HEAD_DIM : (head + 1) * HEAD_DIM]
            outgrads[part, place, :] = outgrad[:, head * HEAD_DIM : (head + 1) * HEAD_DIM]
            norms[part, :, place] = norm[head : head + 1, :]
            dots[part, :, place] = dot[head : head + 1, :]
    data = (queries, outgrads, norms, dots, starts_rows)

    @pl.loop(0, parts)
    def _(part):
        def store(key_term, value_term, query_term):
            own_terms[0, :, columns(part)] = key_term
            own_terms[1, :, columns(part)] = value_term
            query_acc[part] = query_term

        block_terms(tok, 0, part, block, data, store)


def more_kernel(first, spans, starts, *refs):
    data, acc_in, blocks = refs[:5], refs[5], refs[6:-3]
    terms, query_acc, window = refs[-3:]
    tok = lax.axis_index("tok")
    parts = query_acc.shape[0]
    count = jnp.clip(blocks_read(tok, spans, starts) - first, 0, len(blocks))
    query_acc[...] = acc_in[...]
    for slot, block in enumerate(blocks):
        window[slot] = block[...]

        @pl.when(slot >= count)
        def _():
            terms[slot] = jnp.zeros(terms.shape[1:], terms.dtype)

    @pl.loop(0, count * parts)
    def _(step):
        slot, part = step // parts, step % parts

        def store(key_term, value_term, query_term):
            terms[slot, 0, :, columns(part)] = key_term.astype(terms.dtype)
            terms[slot, 1, :, columns(part)] = value_term.astype(terms.dtype)
            query_acc[part] += query_term

        block_terms(tok, first + slot, part, window.at[slot], data, store)


def turn_kernel(acc, query_grad):
    group = acc.shape[2] // QBLOCK
    head_scale = 1.0 / math.sqrt(HEAD_DIM)
    for part in range(acc.shape[0]):
        for member in range(group):
            head = part * group + member
            total = acc[part, :, member * QBLOCK : (member + 1) * QBLOCK] * head_scale
            query_grad[:, head * HEAD_DIM : (head + 1) * HEAD_DIM] = total.astype(query_grad.dtype).T


def sum_kernel(own, *refs):
    arrived, (key_grad, value_grad) = refs[:-2], refs[-2:]
    for which, out in enumerate((key_grad, value_grad)):
        total = own[which]
        for term in arrived:
            total = total + term[which].astype(jnp.float32)
        out[...] = total.astype(out.dtype)


def cost(items, columns_here):
    return pl.CostEstimate(
        flops=items * 10 * QBLOCK * QBLOCK * columns_here,
        bytes_accessed=4 * 1024 * 1024,
        transcendentals=items * QBLOCK * columns_here,
    )


def per_device(query, keys, values, out_grad, log_norm, row_dot, doc_start, spans):
    toks, heads = lax.axis_size("tok"), lax.axis_size("head")
    key_cols = keys.shape[1] // heads
    parts = key_cols // HEAD_DIM
    rows = query.shape[1] // parts
    terms = (2, QBLOCK, key_cols)
    f32, bf16 = jnp.float32, jnp.bfloat16
    starts_rows = doc_start.reshape(-1, QBLOCK)
    shares, case = pack(spans, doc_start, keys, values, heads)
    own = lax.all_to_all(shares, "head", split_axis=0, concat_axis=0)

    def own_part(query, out_grad, log_norm, row_dot, starts_rows, own):
        return pl.pallas_call(
            own_kernel,
            out_shape=(
                jax.ShapeDtypeStruct(terms, f32),
                jax.ShapeDtypeStruct((parts, HEAD_DIM, rows), f32),
                jax.ShapeDtypeStruct((parts, rows, HEAD_DIM), bf16),
                jax.ShapeDtypeStruct((parts, rows, HEAD_DIM), bf16),
                jax.ShapeDtypeStruct((parts, 1, rows), f32),
                jax.ShapeDtypeStruct((parts, 1, rows), f32),
            ),
            in_specs=[VMEM] * 6,
            out_specs=(VMEM,) * 6,
            compiler_params=LARGE,
            cost_estimate=cost(1, query.shape[1]),
            name="own_grads",
        )(query, out_grad, log_norm, row_dot, starts_rows, own)

    def more_part(first, spans, doc_start, data, acc, blocks):
        return pl.pallas_call(
            functools.partial(more_kernel, first),
            out_shape=(
                jax.ShapeDtypeStruct((len(blocks), *terms), bf16),
                jax.ShapeDtypeStruct(acc.shape, acc.dtype),
            ),
            in_specs=[SMEM, SMEM] + [VMEM] * (6 + len(blocks)),
            out_specs=(VMEM,) * 2,
            scratch_shapes=[pltpu.VMEM((len(blocks), *own.shape), own.dtype)],
            compiler_params=LARGE,
            cost_estimate=cost(len(blocks), query.shape[1]),
            name=f"grads_from_{first}",
        )(spans, doc_start, *data, acc, *blocks)

    def branch(far_targets):
        far_steps = [steps for steps in range(NEAR + 1, REACH + 1) if far_targets]

        def targets_of(steps):
            return [target for target in far_targets if target >= steps]

        def run(query, out_grad, log_norm, row_dot, starts_rows, own, spans, doc_start):
            near = [shifted(own, steps) for steps in range(1, NEAR + 1)]
            far = [
                shifted(own, steps, targets_of(steps)) if targets_of(steps) else own
                for steps in far_steps
            ]
            own_terms, acc, *data = own_part(query, out_grad, log_norm, row_dot, starts_rows, own)
            data.append(starts_rows)
            near_terms, acc = more_part(1, spans, doc_start, data, acc, near)
            back = [
                shifted(near_terms[steps - 1], -steps) for steps in range(1, NEAR + 1)
            ]
            if far_steps:
                far_terms, acc = more_part(NEAR + 1, spans, doc_start, data, acc, far)
                for place, steps in enumerate(far_steps):
                    targets = [target - steps for target in targets_of(steps)]
                    if targets:
                        back.append(shifted(far_terms[place], -steps, targets))
            query_grad = pl.pallas_call(
                turn_kernel,
                out_shape=jax.ShapeDtypeStruct(query.shape, bf16),
                in_specs=[VMEM],
                out_specs=VMEM,
                compiler_params=SMALL,
                cost_estimate=pl.CostEstimate(
                    flops=query.size * 100, bytes_accessed=query.size * 6, transcendentals=0
                ),
                name="turn_query_grad",
            )(acc)
            key_grad, value_grad = pl.pallas_call(
                sum_kernel,
                out_shape=(jax.ShapeDtypeStruct(terms[1:], bf16),) * 2,
                in_specs=[VMEM] * (1 + len(back)),
                out_specs=(VMEM,) * 2,
                compiler_params=SMALL,
                name="sum_terms",
            )(own_terms, *back)
            return query_grad, key_grad, value_grad

        return run

    wanted = [[], *([tok] for tok in far_cases(toks)), list(range(NEAR + 1, toks))]
    return lax.switch(
        case[0],
        [branch(targets) for targets in wanted],
        query, out_grad, log_norm, row_dot, starts_rows, own, spans, doc_start,
    )


def solution(mesh):
    in_specs = (
        P("tok", "head"),
        P(("tok", "head"), None),
        P(("tok", "head"), None),
        P("tok", "head"),
        P("head", "tok"),
        P("head", "tok"),
        P(),
        P(),
    )
    out_specs = (P("tok", "head"), P("tok", "head"), P("tok", "head"))
    return jax.shard_map(
        per_device, mesh=mesh, in_specs=in_specs, out_specs=out_specs, check_vma=False
    )
```

```python
import functools
import math

import jax
import jax.numpy as jnp
from jax import lax
from jax.experimental import pallas as pl
from jax.experimental.pallas import tpu as pltpu
from jax.sharding import PartitionSpec as P

HEADS = 64
KV_HEADS = 8
HEAD_DIM = 128
QBLOCK = 128
REACH = 5
NEAR = 2
ABLE_MAX = 5
NT = (((1,), (1,)), ((), ()))
NN = (((1,), (0,)), ((), ()))
HBM = pl.BlockSpec(memory_space=pltpu.HBM)
VMEM = pl.BlockSpec(memory_space=pltpu.VMEM)
SMEM = pl.BlockSpec(memory_space=pltpu.SMEM)
WHOLE = pltpu.CompilerParams(vmem_limit_bytes=60 * 1024 * 1024)
LARGE = pltpu.CompilerParams(vmem_limit_bytes=24 * 1024 * 1024)
SMALL = pltpu.CompilerParams(vmem_limit_bytes=6 * 1024 * 1024)


def matmul(left, right, dims):
    return lax.dot_general(left, right, dims, preferred_element_type=jnp.float32)


def shifted(value, steps, targets=None):
    count = lax.axis_size("tok")
    if targets is None:
        targets = range(max(0, steps), min(count, count + steps))
    return lax.ppermute(value, "tok", [(target - steps, target) for target in targets])


def far_sets(toks):
    able = list(range(NEAR + 1, toks))
    if len(able) > ABLE_MAX:
        return [[], able]
    return [
        [tok for place, tok in enumerate(able) if chosen >> place & 1]
        for chosen in range(1 << len(able))
    ]


def blocks_read(tok, spans, starts):
    lowest = starts[tok * QBLOCK] // QBLOCK
    return jnp.minimum(spans[tok], tok - lowest + 1)


def pack_kernel(keys, values, shares, sems):
    heads, key_cols = shares.shape[0], shares.shape[-1]
    copies = [
        pltpu.make_async_copy(
            source.at[:, pl.ds(head * key_cols, key_cols)],
            shares.at[head, which],
            sems.at[head, which],
        )
        for head in range(heads)
        for which, source in enumerate((keys, values))
    ]
    for copy in copies:
        copy.start()
    for copy in copies:
        copy.wait()


def pack(keys, values, heads):
    rows, key_cols = keys.shape[0], keys.shape[1] // heads
    return pl.pallas_call(
        pack_kernel,
        out_shape=jax.ShapeDtypeStruct((heads, 2, rows, key_cols), keys.dtype),
        in_specs=[HBM, HBM],
        out_specs=HBM,
        scratch_shapes=[pltpu.SemaphoreType.DMA((heads, 2))],
        compiler_params=WHOLE,
        name="pack_shares",
    )(keys, values)


def case_kernel(sets, spans, starts, case):
    toks = spans.shape[0]

    def far(tok):
        return blocks_read(tok, spans, starts) > NEAR + 1

    if sets == 2:
        any_far = lax.fori_loop(0, toks, lambda tok, seen: seen | far(tok), False)
        case[0] = any_far.astype(jnp.int32)
    else:
        case[0] = sum(
            far(tok).astype(jnp.int32) << place for place, tok in enumerate(range(NEAR + 1, toks))
        )


def which_case(sets, spans, doc_start):
    return pl.pallas_call(
        functools.partial(case_kernel, sets),
        out_shape=jax.ShapeDtypeStruct((1,), jnp.int32),
        in_specs=[SMEM, SMEM],
        out_specs=SMEM,
        name="which_case",
    )(spans, doc_start)


def columns(head):
    return pl.ds(pl.multiple_of(head * HEAD_DIM, HEAD_DIM), HEAD_DIM)


def block_terms(part, allowed, blocks, data, store):
    queries, outgrads, norm, dot = data
    head_scale = 1.0 / math.sqrt(HEAD_DIM)
    heads = queries.shape[1] // QBLOCK
    allowed = jnp.concatenate([allowed] * heads, axis=1)
    keys, values = (
        jnp.concatenate(
            [
                block[share, which, :, columns(part)]
                for block in blocks
                for share in range(block.shape[0])
            ],
            axis=0,
        )
        for which in range(2)
    )
    scores = matmul(keys, queries[part], NT) * head_scale
    probs = jnp.where(allowed, jnp.exp(scores - norm[part]), 0.0)
    value_term = matmul(probs.astype(jnp.bfloat16), outgrads[part], NN)
    prob_grad = matmul(values, outgrads[part], NT)
    score_grad = (probs * (prob_grad - dot[part])).astype(jnp.bfloat16)
    key_term = matmul(score_grad, queries[part], NN)
    query_term = matmul(keys.T, score_grad, NN)
    store(key_term * head_scale, value_term, query_term)


def stage_kernel(
    spans, query, outgrad, norm, dot, starts_rows, queries, outgrads, norms, dots, lower
):
    tok = lax.axis_index("tok")
    parts, rows = queries.shape[:2]
    group = rows // QBLOCK
    for part in range(parts):
        for member in range(group):
            head = part * group + member
            place = slice(member * QBLOCK, (member + 1) * QBLOCK)
            queries[part, place, :] = query[:, head * HEAD_DIM : (head + 1) * HEAD_DIM]
            outgrads[part, place, :] = outgrad[:, head * HEAD_DIM : (head + 1) * HEAD_DIM]
            norms[part, :, place] = norm[head : head + 1, :]
            dots[part, :, place] = dot[head : head + 1, :]
    lower[...] = jnp.maximum(starts_rows[pl.ds(tok, 1), :], (tok - spans[tok] + 1) * QBLOCK)


def own_kernel(queries, outgrads, norms, dots, lower, block, own_terms, query_acc):
    tok = lax.axis_index("tok")
    key_row = lax.broadcasted_iota(jnp.int32, (QBLOCK, QBLOCK), 0)
    query_col = lax.broadcasted_iota(jnp.int32, (QBLOCK, QBLOCK), 1)
    allowed = (key_row + tok * QBLOCK >= lower[...]) & (key_row <= query_col)

    @pl.loop(0, query_acc.shape[0])
    def _(part):
        def store(key_term, value_term, query_term):
            own_terms[0, :, columns(part)] = key_term
            own_terms[1, :, columns(part)] = value_term
            query_acc[part] = query_term

        block_terms(part, allowed, [block], (queries, outgrads, norms, dots), store)


def more_kernel(first, *refs):
    data, lower, acc_in, blocks = refs[:4], refs[4], refs[5], refs[6:-2]
    terms, query_acc = refs[-2:]
    count = len(blocks)
    end = (lax.axis_index("tok") - first + 1) * QBLOCK
    read = jnp.min(lower[...]) < end

    @pl.when(jnp.logical_not(read))
    def _():
        terms[...] = jnp.zeros(terms.shape, terms.dtype)
        query_acc[...] = acc_in[...]

    @pl.when(read)
    def _():
        shape = (count * QBLOCK, QBLOCK)
        key_row = lax.broadcasted_iota(jnp.int32, shape, 0)
        allowed = key_row + (end - count * QBLOCK) >= lower[...]

        @pl.loop(0, acc_in.shape[0])
        def _(part):
            def store(key_term, value_term, query_term):
                for slot in range(count):
                    rows = slice((count - 1 - slot) * QBLOCK, (count - slot) * QBLOCK)
                    terms[slot, 0, :, columns(part)] = key_term[rows].astype(terms.dtype)
                    terms[slot, 1, :, columns(part)] = value_term[rows].astype(terms.dtype)
                query_acc[part] = acc_in[part] + query_term

            block_terms(part, allowed, blocks[::-1], data, store)


def turn_kernel(acc, query_grad, turned, sems):
    group = acc.shape[2] // QBLOCK
    head_scale = 1.0 / math.sqrt(HEAD_DIM)
    copies = []
    for part in range(acc.shape[0]):
        for member in range(group):
            head = part * group + member
            total = acc[part, :, member * QBLOCK : (member + 1) * QBLOCK] * head_scale
            turned[:, head * HEAD_DIM : (head + 1) * HEAD_DIM] = total.astype(turned.dtype).T
        place = pl.ds(part * group * HEAD_DIM, group * HEAD_DIM)
        copies.append(
            pltpu.make_async_copy(turned.at[:, place], query_grad.at[:, place], sems.at[part])
        )
        copies[-1].start()
    for copy in copies:
        copy.wait()


def sum_kernel(own, *refs):
    arrived, (key_grad, value_grad, totals, sems) = refs[:-4], refs[-4:]
    copies = []
    for which, out in enumerate((key_grad, value_grad)):
        total = own[which]
        for term in arrived:
            total = total + term[which].astype(jnp.float32)
        totals[which] = total.astype(totals.dtype)
        copies.append(pltpu.make_async_copy(totals.at[which], out, sems.at[which]))
        copies[-1].start()
    for copy in copies:
        copy.wait()


def cost(items, columns_here):
    return pl.CostEstimate(
        flops=items * 10 * QBLOCK * QBLOCK * columns_here,
        bytes_accessed=4 * 1024 * 1024,
        transcendentals=items * QBLOCK * columns_here,
    )


def per_device(query, keys, values, out_grad, log_norm, row_dot, doc_start, spans):
    toks, heads = lax.axis_size("tok"), lax.axis_size("head")
    key_cols = keys.shape[1] // heads
    parts = key_cols // HEAD_DIM
    rows = query.shape[1] // parts
    terms = (2, QBLOCK, key_cols)
    f32, bf16 = jnp.float32, jnp.bfloat16
    starts_rows = doc_start.reshape(-1, QBLOCK)
    sets = far_sets(toks)
    shares = pack(keys, values, heads)
    shares, spans_after = lax.optimization_barrier((shares, spans))
    case = which_case(len(sets), spans_after, doc_start)
    own = lax.all_to_all(shares, "head", split_axis=0, concat_axis=0)

    data = pl.pallas_call(
        stage_kernel,
        out_shape=(
            jax.ShapeDtypeStruct((parts, rows, HEAD_DIM), bf16),
            jax.ShapeDtypeStruct((parts, rows, HEAD_DIM), bf16),
            jax.ShapeDtypeStruct((parts, 1, rows), f32),
            jax.ShapeDtypeStruct((parts, 1, rows), f32),
            jax.ShapeDtypeStruct((1, QBLOCK), jnp.int32),
        ),
        in_specs=[SMEM] + [VMEM] * 5,
        out_specs=(VMEM,) * 5,
        compiler_params=LARGE,
        name="stage_queries",
    )(spans_after, query, out_grad, log_norm, row_dot, starts_rows)

    def own_part(data, own):
        return pl.pallas_call(
            own_kernel,
            out_shape=(
                jax.ShapeDtypeStruct(terms, f32),
                jax.ShapeDtypeStruct((parts, HEAD_DIM, rows), f32),
            ),
            in_specs=[VMEM] * 6,
            out_specs=(VMEM,) * 2,
            compiler_params=LARGE,
            cost_estimate=cost(1, query.shape[1]),
            name="own_grads",
        )(*data, own)

    def more_part(first, data, acc, blocks):
        return pl.pallas_call(
            functools.partial(more_kernel, first),
            out_shape=(
                jax.ShapeDtypeStruct((len(blocks), *terms), bf16),
                jax.ShapeDtypeStruct(acc.shape, acc.dtype),
            ),
            in_specs=[VMEM] * (6 + len(blocks)),
            out_specs=(VMEM,) * 2,
            compiler_params=LARGE,
            cost_estimate=cost(len(blocks), query.shape[1]),
            name=f"grads_from_{first}",
        )(*data, acc, *blocks)

    def branch(far_targets):
        far_steps = [steps for steps in range(NEAR + 1, REACH + 1) if far_targets]

        def targets_of(steps):
            return [target for target in far_targets if target >= steps]

        def run(data, own):
            near = [shifted(own, steps) for steps in range(1, NEAR + 1)]
            far = [
                shifted(own, steps, targets_of(steps)) if targets_of(steps) else own
                for steps in far_steps
            ]
            own_terms, acc = own_part(data, own)
            near_terms, acc = more_part(1, data, acc, near)
            back = [
                shifted(near_terms[steps - 1], -steps) for steps in range(1, NEAR + 1)
            ]
            for steps, arrived in zip(far_steps, far):
                targets = [target - steps for target in targets_of(steps)]
                if targets:
                    far_terms, acc = more_part(steps, data, acc, [arrived])
                    back.append(shifted(far_terms[0], -steps, targets))
            query_grad = pl.pallas_call(
                turn_kernel,
                out_shape=jax.ShapeDtypeStruct(query.shape, bf16),
                in_specs=[VMEM],
                out_specs=HBM,
                scratch_shapes=[pltpu.VMEM(query.shape, bf16), pltpu.SemaphoreType.DMA((parts,))],
                compiler_params=SMALL,
                cost_estimate=pl.CostEstimate(
                    flops=query.size * 100, bytes_accessed=query.size * 6, transcendentals=0
                ),
                name="turn_query_grad",
            )(acc)
            key_grad, value_grad = pl.pallas_call(
                sum_kernel,
                out_shape=(jax.ShapeDtypeStruct(terms[1:], bf16),) * 2,
                in_specs=[VMEM] * (1 + len(back)),
                out_specs=(HBM,) * 2,
                scratch_shapes=[pltpu.VMEM(terms, bf16), pltpu.SemaphoreType.DMA((2,))],
                compiler_params=SMALL,
                name="sum_terms",
            )(own_terms, *back)
            return query_grad, key_grad, value_grad

        return run

    return lax.switch(
        case[0],
        [branch(targets) for targets in sets],
        data,
        own,
    )


def solution(mesh):
    in_specs = (
        P("tok", "head"),
        P(("tok", "head"), None),
        P(("tok", "head"), None),
        P("tok", "head"),
        P("head", "tok"),
        P("head", "tok"),
        P(),
        P(),
    )
    out_specs = (P("tok", "head"), P("tok", "head"), P("tok", "head"))
    return jax.shard_map(
        per_device, mesh=mesh, in_specs=in_specs, out_specs=out_specs, check_vma=False
    )
```

```python
import functools
import math

import jax
import jax.numpy as jnp
from jax import lax
from jax.experimental import pallas as pl
from jax.experimental.pallas import tpu as pltpu
from jax.sharding import PartitionSpec as P

HEADS = 64
KV_HEADS = 8
HEAD_DIM = 128
QBLOCK = 128
REACH = 5
NEAR = 2
ABLE_MAX = 5
NT = (((1,), (1,)), ((), ()))
NN = (((1,), (0,)), ((), ()))
HBM = pl.BlockSpec(memory_space=pltpu.HBM)
VMEM = pl.BlockSpec(memory_space=pltpu.VMEM)
SMEM = pl.BlockSpec(memory_space=pltpu.SMEM)
WHOLE = pltpu.CompilerParams(vmem_limit_bytes=60 * 1024 * 1024)
STAGE = pltpu.CompilerParams(vmem_limit_bytes=56 * 1024 * 1024)
LARGE = pltpu.CompilerParams(vmem_limit_bytes=24 * 1024 * 1024)
SMALL = pltpu.CompilerParams(vmem_limit_bytes=6 * 1024 * 1024)


def matmul(left, right, dims):
    return lax.dot_general(left, right, dims, preferred_element_type=jnp.float32)


def shifted(value, steps, targets=None):
    count = lax.axis_size("tok")
    if targets is None:
        targets = range(max(0, steps), min(count, count + steps))
    return lax.ppermute(value, "tok", [(target - steps, target) for target in targets])


def far_sets(toks):
    able = list(range(NEAR + 1, toks))
    if len(able) > ABLE_MAX:
        return {0: [], 1: able}
    sets = {}
    for chosen in range(1 << len(able)):
        targets = [tok for place, tok in enumerate(able) if chosen >> place & 1]
        if len(targets) <= 2 or targets == able:
            sets[chosen] = targets
    return sets


def choose(case, numbers, branches, operands):
    if len(branches) == 1:
        return branches[0](*operands)
    middle = len(branches) // 2

    def upper(*operands):
        return choose(case, numbers[middle:], branches[middle:], operands)

    def lower(*operands):
        return choose(case, numbers[:middle], branches[:middle], operands)

    return lax.cond(case < numbers[middle], lower, upper, *operands)


def blocks_read(tok, spans, starts):
    lowest = starts[tok * QBLOCK] // QBLOCK
    return jnp.minimum(spans[tok], tok - lowest + 1)


def pack_kernel(keys, values, shares):
    heads, key_cols = shares.shape[0], shares.shape[-1]
    for head in range(heads):
        shares[head, 0] = keys[:, head * key_cols : (head + 1) * key_cols]
        shares[head, 1] = values[:, head * key_cols : (head + 1) * key_cols]


def pack(keys, values, heads):
    rows, key_cols = keys.shape[0], keys.shape[1] // heads
    return pl.pallas_call(
        pack_kernel,
        out_shape=jax.ShapeDtypeStruct((heads, 2, rows, key_cols), keys.dtype),
        in_specs=[VMEM, VMEM],
        out_specs=VMEM,
        compiler_params=WHOLE,
        name="pack_shares",
    )(keys, values)


def case_kernel(sets, spans, starts, case):
    toks = spans.shape[0]

    def far(tok):
        return blocks_read(tok, spans, starts) > NEAR + 1

    if sets == 2:
        any_far = lax.fori_loop(0, toks, lambda tok, seen: seen | far(tok), False)
        case[0] = any_far.astype(jnp.int32)
    else:
        able = toks - NEAR - 1
        bits = [far(NEAR + 1 + place).astype(jnp.int32) for place in range(able)]
        chosen = sum(bit << place for place, bit in enumerate(bits))
        case[0] = jnp.where(sum(bits) > 2, (1 << able) - 1, chosen)


def which_case(sets, spans, doc_start):
    return pl.pallas_call(
        functools.partial(case_kernel, sets),
        out_shape=jax.ShapeDtypeStruct((1,), jnp.int32),
        in_specs=[SMEM, SMEM],
        out_specs=SMEM,
        compiler_params=WHOLE,
        name="which_case",
    )(spans, doc_start)


def columns(head):
    return pl.ds(pl.multiple_of(head * HEAD_DIM, HEAD_DIM), HEAD_DIM)


def block_terms(part, allowed, blocks, data, store):
    queries, outgrads, norm, dot = data
    head_scale = 1.0 / math.sqrt(HEAD_DIM)
    heads = queries.shape[1] // QBLOCK
    allowed = jnp.concatenate([allowed] * heads, axis=1)
    keys, values = (
        jnp.concatenate(
            [
                block[share, which, :, columns(part)]
                for block in blocks
                for share in range(block.shape[0])
            ],
            axis=0,
        )
        for which in range(2)
    )
    scores = matmul(keys, queries[part], NT) * head_scale
    probs = jnp.where(allowed, jnp.exp(scores - norm[part]), 0.0)
    value_term = matmul(probs.astype(jnp.bfloat16), outgrads[part], NN)
    prob_grad = matmul(values, outgrads[part], NT)
    score_grad = (probs * (prob_grad - dot[part])).astype(jnp.bfloat16)
    key_term = matmul(score_grad, queries[part], NN)
    query_term = matmul(keys.T, score_grad, NN)
    store(key_term * head_scale, value_term, query_term)


def stage_kernel(
    spans, query, outgrad, norm, dot, starts_rows, queries, outgrads, norms, dots, lower
):
    tok = lax.axis_index("tok")
    parts, rows = queries.shape[:2]
    group = rows // QBLOCK
    for part in range(parts):
        for member in range(group):
            head = part * group + member
            place = slice(member * QBLOCK, (member + 1) * QBLOCK)
            queries[part, place, :] = query[:, head * HEAD_DIM : (head + 1) * HEAD_DIM]
            outgrads[part, place, :] = outgrad[:, head * HEAD_DIM : (head + 1) * HEAD_DIM]
            norms[part, :, place] = norm[head : head + 1, :]
            dots[part, :, place] = dot[head : head + 1, :]
    lower[...] = jnp.maximum(starts_rows[pl.ds(tok, 1), :], (tok - spans[tok] + 1) * QBLOCK)


def own_kernel(queries, outgrads, norms, dots, lower, block, own_terms, query_acc):
    tok = lax.axis_index("tok")
    key_row = lax.broadcasted_iota(jnp.int32, (QBLOCK, QBLOCK), 0)
    query_col = lax.broadcasted_iota(jnp.int32, (QBLOCK, QBLOCK), 1)
    allowed = (key_row + tok * QBLOCK >= lower[...]) & (key_row <= query_col)

    @pl.loop(0, query_acc.shape[0])
    def _(part):
        def store(key_term, value_term, query_term):
            own_terms[0, :, columns(part)] = key_term
            own_terms[1, :, columns(part)] = value_term
            query_acc[part] = query_term

        block_terms(part, allowed, [block], (queries, outgrads, norms, dots), store)


def more_kernel(first, *refs):
    data, lower, acc_in, blocks = refs[:4], refs[4], refs[5], refs[6:-2]
    terms, query_acc = refs[-2:]
    count = len(blocks)
    end = (lax.axis_index("tok") - first + 1) * QBLOCK
    read = jnp.min(lower[...]) < end

    @pl.when(jnp.logical_not(read))
    def _():
        terms[...] = jnp.zeros(terms.shape, terms.dtype)
        query_acc[...] = acc_in[...]

    @pl.when(read)
    def _():
        shape = (count * QBLOCK, QBLOCK)
        key_row = lax.broadcasted_iota(jnp.int32, shape, 0)
        allowed = key_row + (end - count * QBLOCK) >= lower[...]

        @pl.loop(0, acc_in.shape[0])
        def _(part):
            def store(key_term, value_term, query_term):
                for slot in range(count):
                    rows = slice((count - 1 - slot) * QBLOCK, (count - slot) * QBLOCK)
                    terms[slot, 0, :, columns(part)] = key_term[rows].astype(terms.dtype)
                    terms[slot, 1, :, columns(part)] = value_term[rows].astype(terms.dtype)
                query_acc[part] = acc_in[part] + query_term

            block_terms(part, allowed, blocks[::-1], data, store)


def turn_kernel(acc, query_grad, turned, sems):
    group = acc.shape[2] // QBLOCK
    head_scale = 1.0 / math.sqrt(HEAD_DIM)
    copies = []
    for part in range(acc.shape[0]):
        for member in range(group):
            head = part * group + member
            total = acc[part, :, member * QBLOCK : (member + 1) * QBLOCK] * head_scale
            turned[:, head * HEAD_DIM : (head + 1) * HEAD_DIM] = total.astype(turned.dtype).T
        place = pl.ds(part * group * HEAD_DIM, group * HEAD_DIM)
        copies.append(
            pltpu.make_async_copy(turned.at[:, place], query_grad.at[:, place], sems.at[part])
        )
        copies[-1].start()
    for copy in copies:
        copy.wait()


def sum_kernel(own, *refs):
    arrived, (key_grad, value_grad, totals, sems) = refs[:-4], refs[-4:]
    copies = []
    for which, out in enumerate((key_grad, value_grad)):
        total = own[which]
        for term in arrived:
            total = total + term[which].astype(jnp.float32)
        totals[which] = total.astype(totals.dtype)
        copies.append(pltpu.make_async_copy(totals.at[which], out, sems.at[which]))
        copies[-1].start()
    for copy in copies:
        copy.wait()


def cost(items, columns_here):
    return pl.CostEstimate(
        flops=items * 10 * QBLOCK * QBLOCK * columns_here,
        bytes_accessed=4 * 1024 * 1024,
        transcendentals=items * QBLOCK * columns_here,
    )


def per_device(query, keys, values, out_grad, log_norm, row_dot, doc_start, spans):
    toks, heads = lax.axis_size("tok"), lax.axis_size("head")
    key_cols = keys.shape[1] // heads
    parts = key_cols // HEAD_DIM
    rows = query.shape[1] // parts
    terms = (2, QBLOCK, key_cols)
    f32, bf16 = jnp.float32, jnp.bfloat16
    starts_rows = doc_start.reshape(-1, QBLOCK)
    sets = far_sets(toks)
    shares = pack(keys, values, heads)
    shares, spans_after = lax.optimization_barrier((shares, spans))
    case = which_case(len(sets), spans_after, doc_start)
    own = lax.all_to_all(shares, "head", split_axis=0, concat_axis=0)

    data = pl.pallas_call(
        stage_kernel,
        out_shape=(
            jax.ShapeDtypeStruct((parts, rows, HEAD_DIM), bf16),
            jax.ShapeDtypeStruct((parts, rows, HEAD_DIM), bf16),
            jax.ShapeDtypeStruct((parts, 1, rows), f32),
            jax.ShapeDtypeStruct((parts, 1, rows), f32),
            jax.ShapeDtypeStruct((1, QBLOCK), jnp.int32),
        ),
        in_specs=[SMEM] + [VMEM] * 5,
        out_specs=(VMEM,) * 5,
        compiler_params=STAGE,
        name="stage_queries",
    )(spans_after, query, out_grad, log_norm, row_dot, starts_rows)

    def own_part(data, own):
        return pl.pallas_call(
            own_kernel,
            out_shape=(
                jax.ShapeDtypeStruct(terms, f32),
                jax.ShapeDtypeStruct((parts, HEAD_DIM, rows), f32),
            ),
            in_specs=[VMEM] * 6,
            out_specs=(VMEM,) * 2,
            compiler_params=LARGE,
            cost_estimate=cost(1, query.shape[1]),
            name="own_grads",
        )(*data, own)

    def more_part(first, data, acc, blocks):
        return pl.pallas_call(
            functools.partial(more_kernel, first),
            out_shape=(
                jax.ShapeDtypeStruct((len(blocks), *terms), bf16),
                jax.ShapeDtypeStruct(acc.shape, acc.dtype),
            ),
            in_specs=[VMEM] * (6 + len(blocks)),
            out_specs=(VMEM,) * 2,
            compiler_params=LARGE,
            cost_estimate=cost(len(blocks), query.shape[1]),
            name=f"grads_from_{first}",
        )(*data, acc, *blocks)

    def branch(far_targets):
        far_steps = [steps for steps in range(NEAR + 1, REACH + 1) if far_targets]

        def targets_of(steps):
            return [target for target in far_targets if target >= steps]

        def run(data, own):
            near = [shifted(own, steps) for steps in range(1, NEAR + 1)]
            far = [
                shifted(own, steps, targets_of(steps)) if targets_of(steps) else own
                for steps in far_steps
            ]
            own_terms, acc = own_part(data, own)
            near_terms, acc = more_part(1, data, acc, near)
            back = [
                shifted(near_terms[steps - 1], -steps) for steps in range(1, NEAR + 1)
            ]
            for steps, arrived in zip(far_steps, far):
                targets = [target - steps for target in targets_of(steps)]
                if targets:
                    far_terms, acc = more_part(steps, data, acc, [arrived])
                    back.append(shifted(far_terms[0], -steps, targets))
            return finish(own_terms, acc, back)

        return run

    def finish(own_terms, acc, back):
        query_grad = pl.pallas_call(
            turn_kernel,
            out_shape=jax.ShapeDtypeStruct(query.shape, bf16),
            in_specs=[VMEM],
            out_specs=HBM,
            scratch_shapes=[pltpu.VMEM(query.shape, bf16), pltpu.SemaphoreType.DMA((parts,))],
            compiler_params=SMALL,
            cost_estimate=pl.CostEstimate(
                flops=query.size * 100, bytes_accessed=query.size * 6, transcendentals=0
            ),
            name="turn_query_grad",
        )(acc)
        key_grad, value_grad = pl.pallas_call(
            sum_kernel,
            out_shape=(jax.ShapeDtypeStruct(terms[1:], bf16),) * 2,
            in_specs=[VMEM] * (1 + len(back)),
            out_specs=(HBM,) * 2,
            scratch_shapes=[pltpu.VMEM(terms, bf16), pltpu.SemaphoreType.DMA((2,))],
            compiler_params=SMALL,
            name="sum_terms",
        )(own_terms, *back)
        return query_grad, key_grad, value_grad

    case = case[0]
    numbered = list(sets.items())
    many = [(number, targets) for number, targets in numbered if len(targets) > 1]

    def several(data, own):
        far_steps = range(NEAR + 1, REACH + 1)
        near = [shifted(own, steps) for steps in range(1, NEAR + 1)]

        def fetch(targets):
            def run(own):
                return tuple(
                    shifted(own, steps, [target for target in targets if target >= steps])
                    for steps in far_steps
                )

            return run

        def give(targets):
            def run(far_terms):
                return tuple(
                    shifted(
                        far_terms[place],
                        -steps,
                        [target - steps for target in targets if target >= steps],
                    )
                    for place, steps in enumerate(far_steps)
                )

            return run

        numbers = [number for number, _ in many]
        far = choose(case, numbers, [fetch(targets) for _, targets in many], (own,))
        own_terms, acc = own_part(data, own)
        near_terms, acc = more_part(1, data, acc, near)
        back = [shifted(near_terms[steps - 1], -steps) for steps in range(1, NEAR + 1)]
        far_terms, acc = more_part(NEAR + 1, data, acc, far)
        back += choose(case, numbers, [give(targets) for _, targets in many], (far_terms,))
        return finish(own_terms, acc, back)

    ones = [branch(targets) for _, targets in numbered if len(targets) == 1]
    first_ones = [number for number, targets in numbered if len(targets) == 1]

    def some(data, own):
        if not ones:
            return several(data, own)
        alone = functools.reduce(jnp.logical_or, [case == number for number in first_ones])
        return lax.cond(
            alone, lambda *args: choose(case, first_ones, ones, args), several, data, own
        )

    return lax.cond(case == 0, branch([]), some, data, own)


def solution(mesh):
    in_specs = (
        P("tok", "head"),
        P(("tok", "head"), None),
        P(("tok", "head"), None),
        P("tok", "head"),
        P("head", "tok"),
        P("head", "tok"),
        P(),
        P(),
    )
    out_specs = (P("tok", "head"), P("tok", "head"), P("tok", "head"))
    return jax.shard_map(
        per_device, mesh=mesh, in_specs=in_specs, out_specs=out_specs, check_vma=False
    )
```

```python
import functools
import math

import jax
import jax.numpy as jnp
from jax import lax
from jax.experimental import pallas as pl
from jax.experimental.pallas import tpu as pltpu
from jax.sharding import PartitionSpec as P

HEADS = 64
KV_HEADS = 8
HEAD_DIM = 128
QBLOCK = 128
REACH = 5
NEAR = 2
ABLE_MAX = 5
NT = (((1,), (1,)), ((), ()))
NN = (((1,), (0,)), ((), ()))
HBM = pl.BlockSpec(memory_space=pltpu.HBM)
VMEM = pl.BlockSpec(memory_space=pltpu.VMEM)
SMEM = pl.BlockSpec(memory_space=pltpu.SMEM)
WHOLE = pltpu.CompilerParams(vmem_limit_bytes=60 * 1024 * 1024)
STAGE = pltpu.CompilerParams(vmem_limit_bytes=56 * 1024 * 1024)
LARGE = pltpu.CompilerParams(vmem_limit_bytes=24 * 1024 * 1024)
SMALL = pltpu.CompilerParams(vmem_limit_bytes=6 * 1024 * 1024)


def matmul(left, right, dims):
    return lax.dot_general(left, right, dims, preferred_element_type=jnp.float32)


def shifted(value, steps, targets=None):
    count = lax.axis_size("tok")
    if targets is None:
        targets = range(max(0, steps), min(count, count + steps))
    return lax.ppermute(value, "tok", [(target - steps, target) for target in targets])


def far_sets(toks):
    able = list(range(NEAR + 1, toks))
    return [[], *([tok] for tok in able if len(able) <= ABLE_MAX), able]


def blocks_read(tok, spans, starts):
    lowest = starts[tok * QBLOCK] // QBLOCK
    return jnp.minimum(spans[tok], tok - lowest + 1)


def case_kernel(sets, spans, starts, case):
    toks = spans.shape[0]

    def far(tok):
        return blocks_read(tok, spans, starts) > NEAR + 1

    def count(tok, seen):
        read = far(tok).astype(jnp.int32)
        return seen[0] + read, seen[1] + read * tok

    total, where = lax.fori_loop(0, toks, count, (jnp.int32(0), jnp.int32(0)))
    several = jnp.int32(sets - 1)
    if sets > 2:
        several = jnp.where(total == 1, where - NEAR, several)
    case[0] = jnp.where(total == 0, 0, several)


def which_case(sets, spans, doc_start):
    return pl.pallas_call(
        functools.partial(case_kernel, sets),
        out_shape=jax.ShapeDtypeStruct((1,), jnp.int32),
        in_specs=[SMEM, SMEM],
        out_specs=SMEM,
        compiler_params=WHOLE,
        name="which_case",
    )(spans, doc_start)


def columns(head):
    return pl.ds(pl.multiple_of(head * HEAD_DIM, HEAD_DIM), HEAD_DIM)


def joined(blocks, which, part):
    return jnp.concatenate(
        [
            block[share, which, :, columns(part)]
            for block in blocks
            for share in range(block.shape[0])
        ],
        axis=0,
    )


def block_terms(part, allowed, blocks, data, store):
    queries, outgrads, norm, dot = data
    head_scale = 1.0 / math.sqrt(HEAD_DIM)
    heads = queries.shape[1] // QBLOCK
    allowed = jnp.concatenate([allowed] * heads, axis=1)
    keys, values = (joined(blocks, which, part) for which in range(2))
    scores = matmul(keys, queries[part], NT) * head_scale
    probs = jnp.where(allowed, jnp.exp(scores - norm[part]), 0.0)
    value_term = matmul(probs.astype(jnp.bfloat16), outgrads[part], NN)
    prob_grad = matmul(values, outgrads[part], NT)
    score_grad = (probs * (prob_grad - dot[part])).astype(jnp.bfloat16)
    key_term = matmul(score_grad, queries[part], NN)
    store(key_term * head_scale, value_term, score_grad)


def stage_kernel(
    spans, query, outgrad, norm, dot, starts_rows, queries, outgrads, norms, dots, lower
):
    tok = lax.axis_index("tok")
    parts, rows = queries.shape[:2]
    group = rows // QBLOCK
    for part in range(parts):
        for member in range(group):
            head = part * group + member
            place = slice(member * QBLOCK, (member + 1) * QBLOCK)
            queries[part, place, :] = query[:, head * HEAD_DIM : (head + 1) * HEAD_DIM]
            outgrads[part, place, :] = outgrad[:, head * HEAD_DIM : (head + 1) * HEAD_DIM]
            norms[part, :, place] = norm[head : head + 1, :]
            dots[part, :, place] = dot[head : head + 1, :]
    lower[...] = jnp.maximum(starts_rows[pl.ds(tok, 1), :], (tok - spans[tok] + 1) * QBLOCK)


def own_kernel(queries, outgrads, norms, dots, lower, block, own_terms, score_grads):
    tok = lax.axis_index("tok")
    key_row = lax.broadcasted_iota(jnp.int32, (QBLOCK, QBLOCK), 0)
    query_col = lax.broadcasted_iota(jnp.int32, (QBLOCK, QBLOCK), 1)
    allowed = (key_row + tok * QBLOCK >= lower[...]) & (key_row <= query_col)

    @pl.loop(0, score_grads.shape[0])
    def _(part):
        def store(key_term, value_term, score_grad):
            own_terms[0, :, columns(part)] = key_term
            own_terms[1, :, columns(part)] = value_term
            score_grads[part] = score_grad

        block_terms(part, allowed, [block], (queries, outgrads, norms, dots), store)


def more_kernel(first, *refs):
    data, lower, blocks = refs[:4], refs[4], refs[5:-2]
    terms, score_grads = refs[-2:]
    count = len(blocks)
    end = (lax.axis_index("tok") - first + 1) * QBLOCK
    read = jnp.min(lower[...]) < end

    @pl.when(jnp.logical_not(read))
    def _():
        terms[...] = jnp.zeros(terms.shape, terms.dtype)
        score_grads[...] = jnp.zeros(score_grads.shape, score_grads.dtype)

    @pl.when(read)
    def _():
        shape = (count * QBLOCK, QBLOCK)
        key_row = lax.broadcasted_iota(jnp.int32, shape, 0)
        allowed = key_row + (end - count * QBLOCK) >= lower[...]

        @pl.loop(0, score_grads.shape[0])
        def _(part):
            def store(key_term, value_term, score_grad):
                for slot in range(count):
                    rows = slice((count - 1 - slot) * QBLOCK, (count - slot) * QBLOCK)
                    terms[slot, 0, :, columns(part)] = key_term[rows].astype(terms.dtype)
                    terms[slot, 1, :, columns(part)] = value_term[rows].astype(terms.dtype)
                score_grads[part] = score_grad

            block_terms(part, allowed, blocks[::-1], data, store)


def query_kernel(counts, *refs):
    score_grads, blocks = refs[: len(counts)], refs[len(counts) : -3]
    query_grad, turned, sems = refs[-3:]
    parts = score_grads[0].shape[0]
    group = score_grads[0].shape[2] // QBLOCK
    head_scale = 1.0 / math.sqrt(HEAD_DIM)
    in_order = []
    for count in counts:
        in_order += blocks[len(in_order) : len(in_order) + count][::-1]
    copies = []
    for part in range(parts):
        keys = joined(in_order, 0, part)
        grads = jnp.concatenate([ref[part] for ref in score_grads], axis=0)
        total = (matmul(keys.T, grads, NN) * head_scale).astype(turned.dtype)
        for member in range(group):
            head = part * group + member
            place = slice(head * HEAD_DIM, (head + 1) * HEAD_DIM)
            turned[:, place] = total[:, member * QBLOCK : (member + 1) * QBLOCK].T
        place = pl.ds(part * group * HEAD_DIM, group * HEAD_DIM)
        copies.append(
            pltpu.make_async_copy(turned.at[:, place], query_grad.at[:, place], sems.at[part])
        )
        copies[-1].start()
    for copy in copies:
        copy.wait()


def sum_kernel(own, *refs):
    arrived, (key_grad, value_grad, totals, sems) = refs[:-4], refs[-4:]
    copies = []
    for which, out in enumerate((key_grad, value_grad)):
        total = own[which]
        for term in arrived:
            total = total + term[which].astype(jnp.float32)
        totals[which] = total.astype(totals.dtype)
        copies.append(pltpu.make_async_copy(totals.at[which], out, sems.at[which]))
        copies[-1].start()
    for copy in copies:
        copy.wait()


def cost(items, columns_here):
    return pl.CostEstimate(
        flops=items * 10 * QBLOCK * QBLOCK * columns_here,
        bytes_accessed=4 * 1024 * 1024,
        transcendentals=items * QBLOCK * columns_here,
    )


def per_device(query, keys, values, out_grad, log_norm, row_dot, doc_start, spans):
    toks, heads = lax.axis_size("tok"), lax.axis_size("head")
    key_cols = keys.shape[1] // heads
    parts = key_cols // HEAD_DIM
    rows = query.shape[1] // parts
    terms = (2, QBLOCK, key_cols)
    f32, bf16 = jnp.float32, jnp.bfloat16
    starts_rows = doc_start.reshape(-1, QBLOCK)
    sets = far_sets(toks)
    shares = jnp.stack([keys, values]).reshape(2, -1, heads, key_cols).transpose(2, 0, 1, 3)
    shares, spans_after = lax.optimization_barrier((shares, spans))
    case = which_case(len(sets), spans_after, doc_start)
    own = lax.all_to_all(shares, "head", split_axis=0, concat_axis=0)

    data = pl.pallas_call(
        stage_kernel,
        out_shape=(
            jax.ShapeDtypeStruct((parts, rows, HEAD_DIM), bf16),
            jax.ShapeDtypeStruct((parts, rows, HEAD_DIM), bf16),
            jax.ShapeDtypeStruct((parts, 1, rows), f32),
            jax.ShapeDtypeStruct((parts, 1, rows), f32),
            jax.ShapeDtypeStruct((1, QBLOCK), jnp.int32),
        ),
        in_specs=[SMEM] + [VMEM] * 5,
        out_specs=(VMEM,) * 5,
        compiler_params=STAGE,
        name="stage_queries",
    )(spans_after, query, out_grad, log_norm, row_dot, starts_rows)

    def own_part(data, own):
        return pl.pallas_call(
            own_kernel,
            out_shape=(
                jax.ShapeDtypeStruct(terms, f32),
                jax.ShapeDtypeStruct((parts, QBLOCK, rows), bf16),
            ),
            in_specs=[VMEM] * 6,
            out_specs=(VMEM,) * 2,
            compiler_params=LARGE,
            cost_estimate=cost(1, query.shape[1]),
            name="own_grads",
        )(*data, own)

    def more_part(first, data, blocks):
        return pl.pallas_call(
            functools.partial(more_kernel, first),
            out_shape=(
                jax.ShapeDtypeStruct((len(blocks), *terms), bf16),
                jax.ShapeDtypeStruct((parts, len(blocks) * QBLOCK, rows), bf16),
            ),
            in_specs=[VMEM] * (5 + len(blocks)),
            out_specs=(VMEM,) * 2,
            compiler_params=LARGE,
            cost_estimate=cost(len(blocks), query.shape[1]),
            name=f"grads_from_{first}",
        )(*data, *blocks)

    def branch(far_targets):
        far_steps = [steps for steps in range(NEAR + 1, REACH + 1) if far_targets]

        def targets_of(steps):
            return [target for target in far_targets if target >= steps]

        def run(data, own):
            near = [shifted(own, steps) for steps in range(1, NEAR + 1)]
            far = [
                shifted(own, steps, targets_of(steps)) if targets_of(steps) else own
                for steps in far_steps
            ]
            own_terms, own_grads = own_part(data, own)
            near_terms, near_grads = more_part(1, data, near)
            grads, blocks = [own_grads, near_grads], [[own], near]
            back = [
                shifted(near_terms[steps - 1], -steps) for steps in range(1, NEAR + 1)
            ]
            for steps, arrived in zip(far_steps, far):
                targets = [target - steps for target in targets_of(steps)]
                if targets:
                    far_terms, far_grads = more_part(steps, data, [arrived])
                    grads.append(far_grads)
                    blocks.append([arrived])
                    back.append(shifted(far_terms[0], -steps, targets))
            return finish(own_terms, back, grads, blocks)

        return run

    def finish(own_terms, back, grads, blocks):
        flat = [block for some in blocks for block in some]
        query_grad = pl.pallas_call(
            functools.partial(query_kernel, [len(some) for some in blocks]),
            out_shape=jax.ShapeDtypeStruct(query.shape, bf16),
            in_specs=[VMEM] * (len(grads) + len(flat)),
            out_specs=HBM,
            scratch_shapes=[pltpu.VMEM(query.shape, bf16), pltpu.SemaphoreType.DMA((parts,))],
            compiler_params=LARGE,
            cost_estimate=pl.CostEstimate(
                flops=len(flat) * 2 * QBLOCK * query.size,
                bytes_accessed=query.size * 6,
                transcendentals=0,
            ),
            name="query_grad",
        )(*grads, *flat)
        key_grad, value_grad = pl.pallas_call(
            sum_kernel,
            out_shape=(jax.ShapeDtypeStruct(terms[1:], bf16),) * 2,
            in_specs=[VMEM] * (1 + len(back)),
            out_specs=(HBM,) * 2,
            scratch_shapes=[pltpu.VMEM(terms, bf16), pltpu.SemaphoreType.DMA((2,))],
            compiler_params=SMALL,
            name="sum_terms",
        )(own_terms, *back)
        return query_grad, key_grad, value_grad

    return lax.switch(case[0], [branch(targets) for targets in sets], data, own)


def solution(mesh):
    in_specs = (
        P("tok", "head"),
        P(("tok", "head"), None),
        P(("tok", "head"), None),
        P("tok", "head"),
        P("head", "tok"),
        P("head", "tok"),
        P(),
        P(),
    )
    out_specs = (P("tok", "head"), P("tok", "head"), P("tok", "head"))
    return jax.shard_map(
        per_device, mesh=mesh, in_specs=in_specs, out_specs=out_specs, check_vma=False
    )
```

```python
import functools
import math

import jax
import jax.numpy as jnp
from jax import lax
from jax.experimental import pallas as pl
from jax.experimental.pallas import tpu as pltpu
from jax.sharding import PartitionSpec as P

HEADS = 64
KV_HEADS = 8
HEAD_DIM = 128
QBLOCK = 128
REACH = 5
NEAR = 2
ABLE_MAX = 5
NT = (((1,), (1,)), ((), ()))
NN = (((1,), (0,)), ((), ()))
HBM = pl.BlockSpec(memory_space=pltpu.HBM)
VMEM = pl.BlockSpec(memory_space=pltpu.VMEM)
SMEM = pl.BlockSpec(memory_space=pltpu.SMEM)
WHOLE = pltpu.CompilerParams(vmem_limit_bytes=60 * 1024 * 1024)
STAGE = pltpu.CompilerParams(vmem_limit_bytes=56 * 1024 * 1024)
LARGE = pltpu.CompilerParams(vmem_limit_bytes=24 * 1024 * 1024)
SMALL = pltpu.CompilerParams(vmem_limit_bytes=6 * 1024 * 1024)


def matmul(left, right, dims):
    return lax.dot_general(left, right, dims, preferred_element_type=jnp.float32)


def shifted(value, steps, targets=None):
    count = lax.axis_size("tok")
    if targets is None:
        targets = range(max(0, steps), min(count, count + steps))
    return lax.ppermute(value, "tok", [(target - steps, target) for target in targets])


def far_sets(toks):
    able = list(range(NEAR + 1, toks))
    return [[], *([tok] for tok in able if len(able) <= ABLE_MAX), able]


def blocks_read(tok, spans, starts):
    lowest = starts[tok * QBLOCK] // QBLOCK
    return jnp.minimum(spans[tok], tok - lowest + 1)


def pack_kernel(keys, values, shares):
    heads, key_cols = shares.shape[0], shares.shape[-1]
    for head in range(heads):
        shares[head, 0] = keys[:, head * key_cols : (head + 1) * key_cols]
        shares[head, 1] = values[:, head * key_cols : (head + 1) * key_cols]


def pack(keys, values, heads):
    rows, key_cols = keys.shape[0], keys.shape[1] // heads
    return pl.pallas_call(
        pack_kernel,
        out_shape=jax.ShapeDtypeStruct((heads, 2, rows, key_cols), keys.dtype),
        in_specs=[VMEM, VMEM],
        out_specs=VMEM,
        compiler_params=WHOLE,
        name="pack_shares",
    )(keys, values)


def case_kernel(sets, spans, starts, case):
    toks = spans.shape[0]

    def far(tok):
        return blocks_read(tok, spans, starts) > NEAR + 1

    def count(tok, seen):
        read = far(tok).astype(jnp.int32)
        return seen[0] + read, seen[1] + read * tok

    total, where = lax.fori_loop(0, toks, count, (jnp.int32(0), jnp.int32(0)))
    several = jnp.int32(sets - 1)
    if sets > 2:
        several = jnp.where(total == 1, where - NEAR, several)
    case[0] = jnp.where(total == 0, 0, several)


def which_case(sets, spans, doc_start):
    return pl.pallas_call(
        functools.partial(case_kernel, sets),
        out_shape=jax.ShapeDtypeStruct((1,), jnp.int32),
        in_specs=[SMEM, SMEM],
        out_specs=SMEM,
        compiler_params=WHOLE,
        name="which_case",
    )(spans, doc_start)


def columns(head):
    return pl.ds(pl.multiple_of(head * HEAD_DIM, HEAD_DIM), HEAD_DIM)


def joined(blocks, which, part):
    return jnp.concatenate(
        [
            block[share, which, :, columns(part)]
            for block in blocks
            for share in range(block.shape[0])
        ],
        axis=0,
    )


def block_terms(part, allowed, blocks, data, store):
    queries, outgrads, norm, dot = data
    head_scale = 1.0 / math.sqrt(HEAD_DIM)
    heads = queries.shape[1] // QBLOCK
    allowed = jnp.concatenate([allowed] * heads, axis=1)
    keys, values = (joined(blocks, which, part) for which in range(2))
    scores = matmul(keys, queries[part], NT) * head_scale
    probs = jnp.where(allowed, jnp.exp(scores - norm[part]), 0.0)
    value_term = matmul(probs.astype(jnp.bfloat16), outgrads[part], NN)
    prob_grad = matmul(values, outgrads[part], NT)
    score_grad = (probs * (prob_grad - dot[part])).astype(jnp.bfloat16)
    key_term = matmul(score_grad, queries[part], NN)
    store(key_term * head_scale, value_term, score_grad)


def stage_kernel(
    spans, query, outgrad, norm, dot, starts_rows, queries, outgrads, norms, dots, lower
):
    tok = lax.axis_index("tok")
    parts, rows = queries.shape[:2]
    group = rows // QBLOCK
    for part in range(parts):
        for member in range(group):
            head = part * group + member
            place = slice(member * QBLOCK, (member + 1) * QBLOCK)
            queries[part, place, :] = query[:, head * HEAD_DIM : (head + 1) * HEAD_DIM]
            outgrads[part, place, :] = outgrad[:, head * HEAD_DIM : (head + 1) * HEAD_DIM]
            norms[part, :, place] = norm[head : head + 1, :]
            dots[part, :, place] = dot[head : head + 1, :]
    lower[...] = jnp.maximum(starts_rows[pl.ds(tok, 1), :], (tok - spans[tok] + 1) * QBLOCK)


def own_kernel(queries, outgrads, norms, dots, lower, block, own_terms, score_grads):
    tok = lax.axis_index("tok")
    key_row = lax.broadcasted_iota(jnp.int32, (QBLOCK, QBLOCK), 0)
    query_col = lax.broadcasted_iota(jnp.int32, (QBLOCK, QBLOCK), 1)
    allowed = (key_row + tok * QBLOCK >= lower[...]) & (key_row <= query_col)

    @pl.loop(0, score_grads.shape[0])
    def _(part):
        def store(key_term, value_term, score_grad):
            own_terms[0, :, columns(part)] = key_term
            own_terms[1, :, columns(part)] = value_term
            score_grads[part] = score_grad

        block_terms(part, allowed, [block], (queries, outgrads, norms, dots), store)


def more_kernel(first, *refs):
    data, lower, blocks = refs[:4], refs[4], refs[5:-2]
    terms, score_grads = refs[-2:]
    count = len(blocks)
    end = (lax.axis_index("tok") - first + 1) * QBLOCK
    read = jnp.min(lower[...]) < end

    @pl.when(jnp.logical_not(read))
    def _():
        terms[...] = jnp.zeros(terms.shape, terms.dtype)
        score_grads[...] = jnp.zeros(score_grads.shape, score_grads.dtype)

    @pl.when(read)
    def _():
        shape = (count * QBLOCK, QBLOCK)
        key_row = lax.broadcasted_iota(jnp.int32, shape, 0)
        allowed = key_row + (end - count * QBLOCK) >= lower[...]

        @pl.loop(0, score_grads.shape[0])
        def _(part):
            def store(key_term, value_term, score_grad):
                for slot in range(count):
                    rows = slice((count - 1 - slot) * QBLOCK, (count - slot) * QBLOCK)
                    terms[slot, 0, :, columns(part)] = key_term[rows].astype(terms.dtype)
                    terms[slot, 1, :, columns(part)] = value_term[rows].astype(terms.dtype)
                score_grads[part] = score_grad

            block_terms(part, allowed, blocks[::-1], data, store)


def query_kernel(counts, *refs):
    score_grads, blocks = refs[: len(counts)], refs[len(counts) : -3]
    query_grad, turned, sems = refs[-3:]
    parts = score_grads[0].shape[0]
    group = score_grads[0].shape[2] // QBLOCK
    head_scale = 1.0 / math.sqrt(HEAD_DIM)
    in_order = []
    for count in counts:
        in_order += blocks[len(in_order) : len(in_order) + count][::-1]
    copies = []
    for part in range(parts):
        keys = joined(in_order, 0, part)
        grads = jnp.concatenate([ref[part] for ref in score_grads], axis=0)
        total = (matmul(keys.T, grads, NN) * head_scale).astype(turned.dtype)
        for member in range(group):
            head = part * group + member
            place = slice(head * HEAD_DIM, (head + 1) * HEAD_DIM)
            turned[:, place] = total[:, member * QBLOCK : (member + 1) * QBLOCK].T
        place = pl.ds(part * group * HEAD_DIM, group * HEAD_DIM)
        copies.append(
            pltpu.make_async_copy(turned.at[:, place], query_grad.at[:, place], sems.at[part])
        )
        copies[-1].start()
    for copy in copies:
        copy.wait()


def sum_kernel(own, *refs):
    arrived, (key_grad, value_grad, totals, sems) = refs[:-4], refs[-4:]
    copies = []
    for which, out in enumerate((key_grad, value_grad)):
        total = own[which]
        for term in arrived:
            total = total + term[which].astype(jnp.float32)
        totals[which] = total.astype(totals.dtype)
        copies.append(pltpu.make_async_copy(totals.at[which], out, sems.at[which]))
        copies[-1].start()
    for copy in copies:
        copy.wait()


def cost(items, columns_here):
    return pl.CostEstimate(
        flops=items * 10 * QBLOCK * QBLOCK * columns_here,
        bytes_accessed=4 * 1024 * 1024,
        transcendentals=items * QBLOCK * columns_here,
    )


def per_device(query, keys, values, out_grad, log_norm, row_dot, doc_start, spans):
    toks, heads = lax.axis_size("tok"), lax.axis_size("head")
    key_cols = keys.shape[1] // heads
    parts = key_cols // HEAD_DIM
    rows = query.shape[1] // parts
    terms = (2, QBLOCK, key_cols)
    f32, bf16 = jnp.float32, jnp.bfloat16
    starts_rows = doc_start.reshape(-1, QBLOCK)
    sets = far_sets(toks)
    shares = pack(keys, values, heads)
    shares, spans_after = lax.optimization_barrier((shares, spans))
    case = which_case(len(sets), spans_after, doc_start)
    own = lax.all_to_all(shares, "head", split_axis=0, concat_axis=0)

    data = pl.pallas_call(
        stage_kernel,
        out_shape=(
            jax.ShapeDtypeStruct((parts, rows, HEAD_DIM), bf16),
            jax.ShapeDtypeStruct((parts, rows, HEAD_DIM), bf16),
            jax.ShapeDtypeStruct((parts, 1, rows), f32),
            jax.ShapeDtypeStruct((parts, 1, rows), f32),
            jax.ShapeDtypeStruct((1, QBLOCK), jnp.int32),
        ),
        in_specs=[SMEM] + [VMEM] * 5,
        out_specs=(VMEM,) * 5,
        compiler_params=STAGE,
        name="stage_queries",
    )(spans_after, query, out_grad, log_norm, row_dot, starts_rows)

    def own_part(data, own):
        return pl.pallas_call(
            own_kernel,
            out_shape=(
                jax.ShapeDtypeStruct(terms, f32),
                jax.ShapeDtypeStruct((parts, QBLOCK, rows), bf16),
            ),
            in_specs=[VMEM] * 6,
            out_specs=(VMEM,) * 2,
            compiler_params=LARGE,
            cost_estimate=cost(1, query.shape[1]),
            name="own_grads",
        )(*data, own)

    def more_part(first, data, blocks):
        return pl.pallas_call(
            functools.partial(more_kernel, first),
            out_shape=(
                jax.ShapeDtypeStruct((len(blocks), *terms), bf16),
                jax.ShapeDtypeStruct((parts, len(blocks) * QBLOCK, rows), bf16),
            ),
            in_specs=[VMEM] * (5 + len(blocks)),
            out_specs=(VMEM,) * 2,
            compiler_params=LARGE,
            cost_estimate=cost(len(blocks), query.shape[1]),
            name=f"grads_from_{first}",
        )(*data, *blocks)

    def branch(far_targets):
        far_steps = [steps for steps in range(NEAR + 1, REACH + 1) if far_targets]

        def targets_of(steps):
            return [target for target in far_targets if target >= steps]

        def run(data, own):
            near = [shifted(own, steps) for steps in range(1, NEAR + 1)]
            far = [
                shifted(own, steps, targets_of(steps)) if targets_of(steps) else own
                for steps in far_steps
            ]
            own_terms, own_grads = own_part(data, own)
            near_terms, near_grads = more_part(1, data, near)
            grads, blocks = [own_grads, near_grads], [[own], near]
            back = []
            for steps, arrived in zip(far_steps, far):
                targets = [target - steps for target in targets_of(steps)]
                if targets:
                    far_terms, far_grads = more_part(steps, data, [arrived])
                    grads.append(far_grads)
                    blocks.append([arrived])
                    back.append(shifted(far_terms[0], -steps, targets))
                    near_terms, _ = lax.optimization_barrier((near_terms, far_terms))
            back += [shifted(near_terms[steps - 1], -steps) for steps in range(1, NEAR + 1)]
            return finish(own_terms, back, grads, blocks)

        return run

    def finish(own_terms, back, grads, blocks):
        flat = [block for some in blocks for block in some]
        query_grad = pl.pallas_call(
            functools.partial(query_kernel, [len(some) for some in blocks]),
            out_shape=jax.ShapeDtypeStruct(query.shape, bf16),
            in_specs=[VMEM] * (len(grads) + len(flat)),
            out_specs=HBM,
            scratch_shapes=[pltpu.VMEM(query.shape, bf16), pltpu.SemaphoreType.DMA((parts,))],
            compiler_params=LARGE,
            cost_estimate=pl.CostEstimate(
                flops=len(flat) * 2 * QBLOCK * query.size,
                bytes_accessed=query.size * 6,
                transcendentals=0,
            ),
            name="query_grad",
        )(*grads, *flat)
        key_grad, value_grad = pl.pallas_call(
            sum_kernel,
            out_shape=(jax.ShapeDtypeStruct(terms[1:], bf16),) * 2,
            in_specs=[VMEM] * (1 + len(back)),
            out_specs=(HBM,) * 2,
            scratch_shapes=[pltpu.VMEM(terms, bf16), pltpu.SemaphoreType.DMA((2,))],
            compiler_params=SMALL,
            name="sum_terms",
        )(own_terms, *back)
        return query_grad, key_grad, value_grad

    return lax.switch(case[0], [branch(targets) for targets in sets], data, own)


def solution(mesh):
    in_specs = (
        P("tok", "head"),
        P(("tok", "head"), None),
        P(("tok", "head"), None),
        P("tok", "head"),
        P("head", "tok"),
        P("head", "tok"),
        P(),
        P(),
    )
    out_specs = (P("tok", "head"), P("tok", "head"), P("tok", "head"))
    return jax.shard_map(
        per_device, mesh=mesh, in_specs=in_specs, out_specs=out_specs, check_vma=False
    )
```

```python
import functools
import math

import jax
import jax.numpy as jnp
from jax import lax
from jax.experimental import pallas as pl
from jax.experimental.pallas import tpu as pltpu
from jax.sharding import PartitionSpec as P

HEADS = 64
KV_HEADS = 8
HEAD_DIM = 128
QBLOCK = 128
REACH = 5
NEAR = 2
ABLE_MAX = 5
NT = (((1,), (1,)), ((), ()))
NN = (((1,), (0,)), ((), ()))
HBM = pl.BlockSpec(memory_space=pltpu.HBM)
VMEM = pl.BlockSpec(memory_space=pltpu.VMEM)
SMEM = pl.BlockSpec(memory_space=pltpu.SMEM)
WHOLE = pltpu.CompilerParams(vmem_limit_bytes=60 * 1024 * 1024)
STAGE = pltpu.CompilerParams(vmem_limit_bytes=56 * 1024 * 1024)
LARGE = pltpu.CompilerParams(vmem_limit_bytes=24 * 1024 * 1024)
SMALL = pltpu.CompilerParams(vmem_limit_bytes=6 * 1024 * 1024)


def matmul(left, right, dims):
    return lax.dot_general(left, right, dims, preferred_element_type=jnp.float32)


def shifted(value, steps, targets=None):
    count = lax.axis_size("tok")
    if targets is None:
        targets = range(max(0, steps), min(count, count + steps))
    return lax.ppermute(value, "tok", [(target - steps, target) for target in targets])


def far_sets(toks):
    able = list(range(NEAR + 1, toks))
    return [[], *([tok] for tok in able if len(able) <= ABLE_MAX), able]


def blocks_read(tok, spans, starts):
    lowest = starts[tok * QBLOCK] // QBLOCK
    return jnp.minimum(spans[tok], tok - lowest + 1)


def pack_kernel(keys, values, shares):
    heads, key_cols = shares.shape[0], shares.shape[-1]
    for head in range(heads):
        shares[head, 0] = keys[:, head * key_cols : (head + 1) * key_cols]
        shares[head, 1] = values[:, head * key_cols : (head + 1) * key_cols]


def pack(keys, values, heads):
    rows, key_cols = keys.shape[0], keys.shape[1] // heads
    return pl.pallas_call(
        pack_kernel,
        out_shape=jax.ShapeDtypeStruct((heads, 2, rows, key_cols), keys.dtype),
        in_specs=[VMEM, VMEM],
        out_specs=VMEM,
        compiler_params=WHOLE,
        name="pack_shares",
    )(keys, values)


def case_kernel(sets, spans, starts, case):
    toks = spans.shape[0]

    def far(tok):
        return blocks_read(tok, spans, starts) > NEAR + 1

    def count(tok, seen):
        read = far(tok).astype(jnp.int32)
        return seen[0] + read, seen[1] + read * tok

    total, where = lax.fori_loop(0, toks, count, (jnp.int32(0), jnp.int32(0)))
    several = jnp.int32(sets - 1)
    if sets > 2:
        several = jnp.where(total == 1, where - NEAR, several)
    case[0] = jnp.where(total == 0, 0, several)


def which_case(sets, spans, doc_start):
    return pl.pallas_call(
        functools.partial(case_kernel, sets),
        out_shape=jax.ShapeDtypeStruct((1,), jnp.int32),
        in_specs=[SMEM, SMEM],
        out_specs=SMEM,
        compiler_params=WHOLE,
        name="which_case",
    )(spans, doc_start)


def columns(head):
    return pl.ds(pl.multiple_of(head * HEAD_DIM, HEAD_DIM), HEAD_DIM)


def joined(blocks, which, part):
    return jnp.concatenate(
        [
            block[share, which, :, columns(part)]
            for block in blocks
            for share in range(block.shape[0])
        ],
        axis=0,
    )


def block_terms(part, allowed, blocks, data, store):
    queries, outgrads, norm, dot = data
    head_scale = 1.0 / math.sqrt(HEAD_DIM)
    heads = queries.shape[1] // QBLOCK
    allowed = jnp.concatenate([allowed] * heads, axis=1)
    keys, values = (joined(blocks, which, part) for which in range(2))
    scores = matmul(keys, queries[part], NT) * head_scale
    probs = jnp.where(allowed, jnp.exp(scores - norm[part]), 0.0)
    value_term = matmul(probs.astype(jnp.bfloat16), outgrads[part], NN)
    prob_grad = matmul(values, outgrads[part], NT)
    score_grad = (probs * (prob_grad - dot[part])).astype(jnp.bfloat16)
    key_term = matmul(score_grad, queries[part], NN)
    store(key_term * head_scale, value_term, score_grad)


def stage_kernel(
    spans, query, outgrad, norm, dot, starts_rows, queries, outgrads, norms, dots, lower
):
    tok = lax.axis_index("tok")
    parts, rows = queries.shape[:2]
    group = rows // QBLOCK
    for part in range(parts):
        for member in range(group):
            head = part * group + member
            place = slice(member * QBLOCK, (member + 1) * QBLOCK)
            queries[part, place, :] = query[:, head * HEAD_DIM : (head + 1) * HEAD_DIM]
            outgrads[part, place, :] = outgrad[:, head * HEAD_DIM : (head + 1) * HEAD_DIM]
            norms[part, :, place] = norm[head : head + 1, :]
            dots[part, :, place] = dot[head : head + 1, :]
    lower[...] = jnp.maximum(starts_rows[pl.ds(tok, 1), :], (tok - spans[tok] + 1) * QBLOCK)


def own_kernel(queries, outgrads, norms, dots, lower, block, own_terms, score_grads):
    tok = lax.axis_index("tok")
    key_row = lax.broadcasted_iota(jnp.int32, (QBLOCK, QBLOCK), 0)
    query_col = lax.broadcasted_iota(jnp.int32, (QBLOCK, QBLOCK), 1)
    allowed = (key_row + tok * QBLOCK >= lower[...]) & (key_row <= query_col)

    @pl.loop(0, score_grads.shape[0])
    def _(part):
        def store(key_term, value_term, score_grad):
            own_terms[0, :, columns(part)] = key_term
            own_terms[1, :, columns(part)] = value_term
            score_grads[part] = score_grad

        block_terms(part, allowed, [block], (queries, outgrads, norms, dots), store)


def more_kernel(first, *refs):
    data, lower, blocks = refs[:4], refs[4], refs[5:-2]
    terms, score_grads = refs[-2:]
    count = len(blocks)
    end = (lax.axis_index("tok") - first + 1) * QBLOCK
    read = jnp.min(lower[...]) < end

    @pl.when(jnp.logical_not(read))
    def _():
        terms[...] = jnp.zeros(terms.shape, terms.dtype)
        score_grads[...] = jnp.zeros(score_grads.shape, score_grads.dtype)

    @pl.when(read)
    def _():
        shape = (count * QBLOCK, QBLOCK)
        key_row = lax.broadcasted_iota(jnp.int32, shape, 0)
        allowed = key_row + (end - count * QBLOCK) >= lower[...]

        @pl.loop(0, score_grads.shape[0])
        def _(part):
            def store(key_term, value_term, score_grad):
                for slot in range(count):
                    rows = slice((count - 1 - slot) * QBLOCK, (count - slot) * QBLOCK)
                    terms[slot, 0, :, columns(part)] = key_term[rows].astype(terms.dtype)
                    terms[slot, 1, :, columns(part)] = value_term[rows].astype(terms.dtype)
                score_grads[part] = score_grad

            block_terms(part, allowed, blocks[::-1], data, store)


def query_kernel(counts, *refs):
    score_grads, blocks = refs[: len(counts)], refs[len(counts) : -3]
    query_grad, turned, sems = refs[-3:]
    parts = score_grads[0].shape[0]
    group = score_grads[0].shape[2] // QBLOCK
    head_scale = 1.0 / math.sqrt(HEAD_DIM)
    in_order = []
    for count in counts:
        in_order += blocks[len(in_order) : len(in_order) + count][::-1]
    width = group * HEAD_DIM

    def copy_out(part):
        place = pl.ds(pl.multiple_of(part * width, width), width)
        return pltpu.make_async_copy(turned.at[:, place], query_grad.at[:, place], sems.at[part])

    @pl.loop(0, parts)
    def _(part):
        keys = joined(in_order, 0, part)
        grads = jnp.concatenate([ref[part] for ref in score_grads], axis=0)
        total = (matmul(keys.T, grads, NN) * head_scale).astype(turned.dtype)
        for member in range(group):
            place = columns(part * group + member)
            turned[:, place] = total[:, member * QBLOCK : (member + 1) * QBLOCK].T
        copy_out(part).start()

    @pl.loop(0, parts)
    def _(part):
        copy_out(part).wait()


def sum_kernel(own, *refs):
    arrived, (key_grad, value_grad, totals, sems) = refs[:-4], refs[-4:]
    copies = []
    for which, out in enumerate((key_grad, value_grad)):
        total = own[which]
        for term in arrived:
            total = total + term[which].astype(jnp.float32)
        totals[which] = total.astype(totals.dtype)
        copies.append(pltpu.make_async_copy(totals.at[which], out, sems.at[which]))
        copies[-1].start()
    for copy in copies:
        copy.wait()


def cost(items, columns_here):
    return pl.CostEstimate(
        flops=items * 10 * QBLOCK * QBLOCK * columns_here,
        bytes_accessed=4 * 1024 * 1024,
        transcendentals=items * QBLOCK * columns_here,
    )


def per_device(query, keys, values, out_grad, log_norm, row_dot, doc_start, spans):
    toks, heads = lax.axis_size("tok"), lax.axis_size("head")
    key_cols = keys.shape[1] // heads
    parts = key_cols // HEAD_DIM
    rows = query.shape[1] // parts
    terms = (2, QBLOCK, key_cols)
    f32, bf16 = jnp.float32, jnp.bfloat16
    starts_rows = doc_start.reshape(-1, QBLOCK)
    sets = far_sets(toks)
    shares = pack(keys, values, heads)
    shares, spans_after = lax.optimization_barrier((shares, spans))
    case = which_case(len(sets), spans_after, doc_start)
    own = lax.all_to_all(shares, "head", split_axis=0, concat_axis=0)

    data = pl.pallas_call(
        stage_kernel,
        out_shape=(
            jax.ShapeDtypeStruct((parts, rows, HEAD_DIM), bf16),
            jax.ShapeDtypeStruct((parts, rows, HEAD_DIM), bf16),
            jax.ShapeDtypeStruct((parts, 1, rows), f32),
            jax.ShapeDtypeStruct((parts, 1, rows), f32),
            jax.ShapeDtypeStruct((1, QBLOCK), jnp.int32),
        ),
        in_specs=[SMEM] + [VMEM] * 5,
        out_specs=(VMEM,) * 5,
        compiler_params=STAGE,
        name="stage_queries",
    )(spans_after, query, out_grad, log_norm, row_dot, starts_rows)

    def own_part(data, own):
        return pl.pallas_call(
            own_kernel,
            out_shape=(
                jax.ShapeDtypeStruct(terms, f32),
                jax.ShapeDtypeStruct((parts, QBLOCK, rows), bf16),
            ),
            in_specs=[VMEM] * 6,
            out_specs=(VMEM,) * 2,
            compiler_params=LARGE,
            cost_estimate=cost(1, query.shape[1]),
            name="own_grads",
        )(*data, own)

    def more_part(first, data, blocks):
        return pl.pallas_call(
            functools.partial(more_kernel, first),
            out_shape=(
                jax.ShapeDtypeStruct((len(blocks), *terms), bf16),
                jax.ShapeDtypeStruct((parts, len(blocks) * QBLOCK, rows), bf16),
            ),
            in_specs=[VMEM] * (5 + len(blocks)),
            out_specs=(VMEM,) * 2,
            compiler_params=LARGE,
            cost_estimate=cost(len(blocks), query.shape[1]),
            name=f"grads_from_{first}",
        )(*data, *blocks)

    def branch(far_targets):
        far_steps = [steps for steps in range(NEAR + 1, REACH + 1) if far_targets]

        def targets_of(steps):
            return [target for target in far_targets if target >= steps]

        def run(data, own):
            near = [shifted(own, steps) for steps in range(1, NEAR + 1)]
            far = [
                shifted(own, steps, targets_of(steps)) if targets_of(steps) else own
                for steps in far_steps
            ]
            own_terms, own_grads = own_part(data, own)
            near_terms, near_grads = more_part(1, data, near)
            grads, blocks = [own_grads, near_grads], [[own], near]
            back = []
            for steps, arrived in zip(far_steps, far):
                targets = [target - steps for target in targets_of(steps)]
                if targets:
                    far_terms, far_grads = more_part(steps, data, [arrived])
                    grads.append(far_grads)
                    blocks.append([arrived])
                    back.append(shifted(far_terms[0], -steps, targets))
                    near_terms, _ = lax.optimization_barrier((near_terms, far_terms))
            back += [shifted(near_terms[steps - 1], -steps) for steps in range(1, NEAR + 1)]
            return finish(own_terms, back, grads, blocks)

        return run

    def finish(own_terms, back, grads, blocks):
        flat = [block for some in blocks for block in some]
        query_grad = pl.pallas_call(
            functools.partial(query_kernel, [len(some) for some in blocks]),
            out_shape=jax.ShapeDtypeStruct(query.shape, bf16),
            in_specs=[VMEM] * (len(grads) + len(flat)),
            out_specs=HBM,
            scratch_shapes=[pltpu.VMEM(query.shape, bf16), pltpu.SemaphoreType.DMA((parts,))],
            compiler_params=LARGE,
            cost_estimate=pl.CostEstimate(
                flops=len(flat) * 2 * QBLOCK * query.size,
                bytes_accessed=query.size * 6,
                transcendentals=0,
            ),
            name="query_grad",
        )(*grads, *flat)
        key_grad, value_grad = pl.pallas_call(
            sum_kernel,
            out_shape=(jax.ShapeDtypeStruct(terms[1:], bf16),) * 2,
            in_specs=[VMEM] * (1 + len(back)),
            out_specs=(HBM,) * 2,
            scratch_shapes=[pltpu.VMEM(terms, bf16), pltpu.SemaphoreType.DMA((2,))],
            compiler_params=SMALL,
            name="sum_terms",
        )(own_terms, *back)
        return query_grad, key_grad, value_grad

    return lax.switch(case[0], [branch(targets) for targets in sets], data, own)


def solution(mesh):
    in_specs = (
        P("tok", "head"),
        P(("tok", "head"), None),
        P(("tok", "head"), None),
        P("tok", "head"),
        P("head", "tok"),
        P("head", "tok"),
        P(),
        P(),
    )
    out_specs = (P("tok", "head"), P("tok", "head"), P("tok", "head"))
    return jax.shard_map(
        per_device, mesh=mesh, in_specs=in_specs, out_specs=out_specs, check_vma=False
    )
```

```python
import functools
import math

import jax
import jax.numpy as jnp
from jax import lax
from jax.experimental import pallas as pl
from jax.experimental.pallas import tpu as pltpu
from jax.sharding import PartitionSpec as P

HEADS = 64
KV_HEADS = 8
HEAD_DIM = 128
QBLOCK = 128
REACH = 5
NEAR = 2
ABLE_MAX = 5
PASS_HEADS = 4
NT = (((1,), (1,)), ((), ()))
NN = (((1,), (0,)), ((), ()))
HBM = pl.BlockSpec(memory_space=pltpu.HBM)
VMEM = pl.BlockSpec(memory_space=pltpu.VMEM)
SMEM = pl.BlockSpec(memory_space=pltpu.SMEM)
WHOLE = pltpu.CompilerParams(vmem_limit_bytes=60 * 1024 * 1024)
STAGE = pltpu.CompilerParams(vmem_limit_bytes=56 * 1024 * 1024)
LARGE = pltpu.CompilerParams(vmem_limit_bytes=24 * 1024 * 1024)
SMALL = pltpu.CompilerParams(vmem_limit_bytes=6 * 1024 * 1024)


def matmul(left, right, dims):
    return lax.dot_general(left, right, dims, preferred_element_type=jnp.float32)


def shifted(value, steps, targets=None):
    count = lax.axis_size("tok")
    if targets is None:
        targets = range(max(0, steps), min(count, count + steps))
    return lax.ppermute(value, "tok", [(target - steps, target) for target in targets])


def far_sets(toks):
    able = list(range(NEAR + 1, toks))
    return [[], *([tok] for tok in able if len(able) <= ABLE_MAX), able]


def blocks_read(tok, spans, starts):
    lowest = starts[tok * QBLOCK] // QBLOCK
    return jnp.minimum(spans[tok], tok - lowest + 1)


def pack_kernel(keys, values, shares):
    heads, key_cols = shares.shape[0], shares.shape[-1]
    for head in range(heads):
        shares[head, 0] = keys[:, head * key_cols : (head + 1) * key_cols]
        shares[head, 1] = values[:, head * key_cols : (head + 1) * key_cols]


def pack(keys, values, heads):
    rows, key_cols = keys.shape[0], keys.shape[1] // heads
    return pl.pallas_call(
        pack_kernel,
        out_shape=jax.ShapeDtypeStruct((heads, 2, rows, key_cols), keys.dtype),
        in_specs=[VMEM, VMEM],
        out_specs=VMEM,
        compiler_params=WHOLE,
        name="pack_shares",
    )(keys, values)


def case_kernel(sets, spans, starts, case):
    toks = spans.shape[0]

    def far(tok):
        return blocks_read(tok, spans, starts) > NEAR + 1

    def count(tok, seen):
        read = far(tok).astype(jnp.int32)
        return seen[0] + read, seen[1] + read * tok

    total, where = lax.fori_loop(0, toks, count, (jnp.int32(0), jnp.int32(0)))
    several = jnp.int32(sets - 1)
    if sets > 2:
        several = jnp.where(total == 1, where - NEAR, several)
    case[0] = jnp.where(total == 0, 0, several)


def which_case(sets, spans, doc_start):
    return pl.pallas_call(
        functools.partial(case_kernel, sets),
        out_shape=jax.ShapeDtypeStruct((1,), jnp.int32),
        in_specs=[SMEM, SMEM],
        out_specs=SMEM,
        compiler_params=WHOLE,
        name="which_case",
    )(spans, doc_start)


def columns(head):
    return pl.ds(pl.multiple_of(head * HEAD_DIM, HEAD_DIM), HEAD_DIM)


def joined(blocks, which, part):
    return jnp.concatenate(
        [
            block[share, which, :, columns(part)]
            for block in blocks
            for share in range(block.shape[0])
        ],
        axis=0,
    )


def block_terms(allowed, blocks, data, sums, score_grads, store):
    queries, outgrads, norm, dot = data
    head_scale = 1.0 / math.sqrt(HEAD_DIM)
    parts, rows = queries.shape[:2]
    heads = min(PASS_HEADS, rows // QBLOCK)
    width = heads * QBLOCK
    passes = rows // width
    allowed = jnp.concatenate([allowed] * heads, axis=1)

    @pl.loop(0, parts * passes)
    def _(step):
        part, turn = step // passes, step % passes
        place = pl.ds(pl.multiple_of(turn * width, width), width)
        keys, values = (joined(blocks, which, part) for which in range(2))
        query_rows, outgrad_rows = queries[part, place, :], outgrads[part, place, :]
        scores = matmul(keys, query_rows, NT) * head_scale
        probs = jnp.where(allowed, jnp.exp(scores - norm[part, :, place]), 0.0)
        value_term = matmul(probs.astype(jnp.bfloat16), outgrad_rows, NN)
        prob_grad = matmul(values, outgrad_rows, NT)
        score_grad = (probs * (prob_grad - dot[part, :, place])).astype(jnp.bfloat16)
        key_term = matmul(score_grad, query_rows, NN)
        score_grads[part, :, place] = score_grad

        @pl.when(turn == 0)
        def _():
            sums[0] = key_term
            sums[1] = value_term

        @pl.when(turn > 0)
        def _():
            sums[0] += key_term
            sums[1] += value_term

        @pl.when(turn == passes - 1)
        def _():
            store(part, sums[0] * head_scale, sums[1])


def stage_kernel(
    spans, query, outgrad, norm, dot, starts_rows, queries, outgrads, norms, dots, lower
):
    tok = lax.axis_index("tok")
    parts, rows = queries.shape[:2]
    group = rows // QBLOCK
    for part in range(parts):
        for member in range(group):
            head = part * group + member
            place = slice(member * QBLOCK, (member + 1) * QBLOCK)
            queries[part, place, :] = query[:, head * HEAD_DIM : (head + 1) * HEAD_DIM]
            outgrads[part, place, :] = outgrad[:, head * HEAD_DIM : (head + 1) * HEAD_DIM]
            norms[part, :, place] = norm[head : head + 1, :]
            dots[part, :, place] = dot[head : head + 1, :]
    lower[...] = jnp.maximum(starts_rows[pl.ds(tok, 1), :], (tok - spans[tok] + 1) * QBLOCK)


def own_kernel(queries, outgrads, norms, dots, lower, block, own_terms, score_grads, sums):
    tok = lax.axis_index("tok")
    key_row = lax.broadcasted_iota(jnp.int32, (QBLOCK, QBLOCK), 0)
    query_col = lax.broadcasted_iota(jnp.int32, (QBLOCK, QBLOCK), 1)
    allowed = (key_row + tok * QBLOCK >= lower[...]) & (key_row <= query_col)

    def store(part, key_term, value_term):
        own_terms[0, :, columns(part)] = key_term
        own_terms[1, :, columns(part)] = value_term

    block_terms(allowed, [block], (queries, outgrads, norms, dots), sums, score_grads, store)


def more_kernel(first, *refs):
    data, lower, blocks = refs[:4], refs[4], refs[5:-3]
    terms, score_grads, sums = refs[-3:]
    count = len(blocks)
    end = (lax.axis_index("tok") - first + 1) * QBLOCK
    read = jnp.min(lower[...]) < end

    @pl.when(jnp.logical_not(read))
    def _():
        terms[...] = jnp.zeros(terms.shape, terms.dtype)
        score_grads[...] = jnp.zeros(score_grads.shape, score_grads.dtype)

    @pl.when(read)
    def _():
        key_row = lax.broadcasted_iota(jnp.int32, (count * QBLOCK, QBLOCK), 0)
        allowed = key_row + (end - count * QBLOCK) >= lower[...]

        def store(part, key_term, value_term):
            for slot in range(count):
                rows = slice((count - 1 - slot) * QBLOCK, (count - slot) * QBLOCK)
                terms[slot, 0, :, columns(part)] = key_term[rows].astype(terms.dtype)
                terms[slot, 1, :, columns(part)] = value_term[rows].astype(terms.dtype)

        block_terms(allowed, blocks[::-1], data, sums, score_grads, store)


def query_kernel(counts, *refs):
    score_grads, blocks = refs[: len(counts)], refs[len(counts) : -3]
    query_grad, turned, sems = refs[-3:]
    parts = score_grads[0].shape[0]
    group = score_grads[0].shape[2] // QBLOCK
    head_scale = 1.0 / math.sqrt(HEAD_DIM)
    in_order = []
    for count in counts:
        in_order += blocks[len(in_order) : len(in_order) + count][::-1]
    width = group * HEAD_DIM

    def copy_out(part):
        place = pl.ds(pl.multiple_of(part * width, width), width)
        return pltpu.make_async_copy(turned.at[:, place], query_grad.at[:, place], sems.at[part])

    @pl.loop(0, parts)
    def _(part):
        keys = joined(in_order, 0, part)
        grads = jnp.concatenate([ref[part] for ref in score_grads], axis=0)
        total = (matmul(keys.T, grads, NN) * head_scale).astype(turned.dtype)
        for member in range(group):
            place = columns(part * group + member)
            turned[:, place] = total[:, member * QBLOCK : (member + 1) * QBLOCK].T
        copy_out(part).start()

    @pl.loop(0, parts)
    def _(part):
        copy_out(part).wait()


def sum_kernel(own, *refs):
    arrived, (key_grad, value_grad, totals, sems) = refs[:-4], refs[-4:]
    copies = []
    for which, out in enumerate((key_grad, value_grad)):
        total = own[which]
        for term in arrived:
            total = total + term[which].astype(jnp.float32)
        totals[which] = total.astype(totals.dtype)
        copies.append(pltpu.make_async_copy(totals.at[which], out, sems.at[which]))
        copies[-1].start()
    for copy in copies:
        copy.wait()


def cost(items, columns_here):
    return pl.CostEstimate(
        flops=items * 10 * QBLOCK * QBLOCK * columns_here,
        bytes_accessed=4 * 1024 * 1024,
        transcendentals=items * QBLOCK * columns_here,
    )


def per_device(query, keys, values, out_grad, log_norm, row_dot, doc_start, spans):
    toks, heads = lax.axis_size("tok"), lax.axis_size("head")
    key_cols = keys.shape[1] // heads
    parts = key_cols // HEAD_DIM
    rows = query.shape[1] // parts
    terms = (2, QBLOCK, key_cols)
    f32, bf16 = jnp.float32, jnp.bfloat16
    starts_rows = doc_start.reshape(-1, QBLOCK)
    sets = far_sets(toks)
    shares = pack(keys, values, heads)
    shares, spans_after = lax.optimization_barrier((shares, spans))
    case = which_case(len(sets), spans_after, doc_start)
    own = lax.all_to_all(shares, "head", split_axis=0, concat_axis=0)

    data = pl.pallas_call(
        stage_kernel,
        out_shape=(
            jax.ShapeDtypeStruct((parts, rows, HEAD_DIM), bf16),
            jax.ShapeDtypeStruct((parts, rows, HEAD_DIM), bf16),
            jax.ShapeDtypeStruct((parts, 1, rows), f32),
            jax.ShapeDtypeStruct((parts, 1, rows), f32),
            jax.ShapeDtypeStruct((1, QBLOCK), jnp.int32),
        ),
        in_specs=[SMEM] + [VMEM] * 5,
        out_specs=(VMEM,) * 5,
        compiler_params=STAGE,
        name="stage_queries",
    )(spans_after, query, out_grad, log_norm, row_dot, starts_rows)

    def own_part(data, own):
        return pl.pallas_call(
            own_kernel,
            out_shape=(
                jax.ShapeDtypeStruct(terms, f32),
                jax.ShapeDtypeStruct((parts, QBLOCK, rows), bf16),
            ),
            in_specs=[VMEM] * 6,
            out_specs=(VMEM,) * 2,
            scratch_shapes=[pltpu.VMEM((2, QBLOCK, HEAD_DIM), f32)],
            compiler_params=LARGE,
            cost_estimate=cost(1, query.shape[1]),
            name="own_grads",
        )(*data, own)

    def more_part(first, data, blocks):
        return pl.pallas_call(
            functools.partial(more_kernel, first),
            out_shape=(
                jax.ShapeDtypeStruct((len(blocks), *terms), bf16),
                jax.ShapeDtypeStruct((parts, len(blocks) * QBLOCK, rows), bf16),
            ),
            in_specs=[VMEM] * (5 + len(blocks)),
            out_specs=(VMEM,) * 2,
            scratch_shapes=[pltpu.VMEM((2, len(blocks) * QBLOCK, HEAD_DIM), f32)],
            compiler_params=LARGE,
            cost_estimate=cost(len(blocks), query.shape[1]),
            name=f"grads_from_{first}",
        )(*data, *blocks)

    def branch(far_targets):
        far_steps = [steps for steps in range(NEAR + 1, REACH + 1) if far_targets]

        def targets_of(steps):
            return [target for target in far_targets if target >= steps]

        def run(data, own):
            near = [shifted(own, steps) for steps in range(1, NEAR + 1)]
            far = [
                shifted(own, steps, targets_of(steps)) if targets_of(steps) else own
                for steps in far_steps
            ]
            own_terms, own_grads = own_part(data, own)
            near_terms, near_grads = more_part(1, data, near)
            grads, blocks = [own_grads, near_grads], [[own], near]
            back = []
            for steps, arrived in zip(far_steps, far):
                targets = [target - steps for target in targets_of(steps)]
                if targets:
                    far_terms, far_grads = more_part(steps, data, [arrived])
                    grads.append(far_grads)
                    blocks.append([arrived])
                    back.append(shifted(far_terms[0], -steps, targets))
                    near_terms, _ = lax.optimization_barrier((near_terms, far_terms))
            back += [shifted(near_terms[steps - 1], -steps) for steps in range(1, NEAR + 1)]
            return finish(own_terms, back, grads, blocks)

        return run

    def finish(own_terms, back, grads, blocks):
        flat = [block for some in blocks for block in some]
        query_grad = pl.pallas_call(
            functools.partial(query_kernel, [len(some) for some in blocks]),
            out_shape=jax.ShapeDtypeStruct(query.shape, bf16),
            in_specs=[VMEM] * (len(grads) + len(flat)),
            out_specs=HBM,
            scratch_shapes=[pltpu.VMEM(query.shape, bf16), pltpu.SemaphoreType.DMA((parts,))],
            compiler_params=LARGE,
            cost_estimate=pl.CostEstimate(
                flops=len(flat) * 2 * QBLOCK * query.size,
                bytes_accessed=query.size * 6,
                transcendentals=0,
            ),
            name="query_grad",
        )(*grads, *flat)
        key_grad, value_grad = pl.pallas_call(
            sum_kernel,
            out_shape=(jax.ShapeDtypeStruct(terms[1:], bf16),) * 2,
            in_specs=[VMEM] * (1 + len(back)),
            out_specs=(HBM,) * 2,
            scratch_shapes=[pltpu.VMEM(terms, bf16), pltpu.SemaphoreType.DMA((2,))],
            compiler_params=SMALL,
            name="sum_terms",
        )(own_terms, *back)
        return query_grad, key_grad, value_grad

    return lax.switch(case[0], [branch(targets) for targets in sets], data, own)


def solution(mesh):
    in_specs = (
        P("tok", "head"),
        P(("tok", "head"), None),
        P(("tok", "head"), None),
        P("tok", "head"),
        P("head", "tok"),
        P("head", "tok"),
        P(),
        P(),
    )
    out_specs = (P("tok", "head"), P("tok", "head"), P("tok", "head"))
    return jax.shard_map(
        per_device, mesh=mesh, in_specs=in_specs, out_specs=out_specs, check_vma=False
    )
```

```python
import functools
import math

import jax
import jax.numpy as jnp
from jax import lax
from jax.experimental import pallas as pl
from jax.experimental.pallas import tpu as pltpu
from jax.sharding import PartitionSpec as P

HEADS = 64
KV_HEADS = 8
HEAD_DIM = 128
QBLOCK = 128
REACH = 5
NEAR = 2
ABLE_MAX = 5
NT = (((1,), (1,)), ((), ()))
NN = (((1,), (0,)), ((), ()))
VMEM = pl.BlockSpec(memory_space=pltpu.VMEM)
SMEM = pl.BlockSpec(memory_space=pltpu.SMEM)
WHOLE = pltpu.CompilerParams(vmem_limit_bytes=60 * 1024 * 1024)
STAGE = pltpu.CompilerParams(vmem_limit_bytes=56 * 1024 * 1024)
LARGE = pltpu.CompilerParams(vmem_limit_bytes=24 * 1024 * 1024)
SMALL = pltpu.CompilerParams(vmem_limit_bytes=6 * 1024 * 1024)


def matmul(left, right, dims):
    return lax.dot_general(left, right, dims, preferred_element_type=jnp.float32)


def shifted(value, steps, targets=None):
    count = lax.axis_size("tok")
    if targets is None:
        targets = range(max(0, steps), min(count, count + steps))
    return lax.ppermute(value, "tok", [(target - steps, target) for target in targets])


def far_sets(toks):
    able = list(range(NEAR + 1, toks))
    return [[], *([tok] for tok in able if len(able) <= ABLE_MAX), able]


def blocks_read(tok, spans, starts):
    lowest = starts[tok * QBLOCK] // QBLOCK
    return jnp.minimum(spans[tok], tok - lowest + 1)


def pack_kernel(keys, values, shares):
    heads, key_cols = shares.shape[0], shares.shape[-1]
    for head in range(heads):
        shares[head, 0] = keys[:, head * key_cols : (head + 1) * key_cols]
        shares[head, 1] = values[:, head * key_cols : (head + 1) * key_cols]


def pack(keys, values, heads):
    rows, key_cols = keys.shape[0], keys.shape[1] // heads
    return pl.pallas_call(
        pack_kernel,
        out_shape=jax.ShapeDtypeStruct((heads, 2, rows, key_cols), keys.dtype),
        in_specs=[VMEM, VMEM],
        out_specs=VMEM,
        compiler_params=WHOLE,
        name="pack_shares",
    )(keys, values)


def case_kernel(sets, spans, starts, case):
    toks = spans.shape[0]

    def far(tok):
        return blocks_read(tok, spans, starts) > NEAR + 1

    def count(tok, seen):
        read = far(tok).astype(jnp.int32)
        return seen[0] + read, seen[1] + read * tok

    total, where = lax.fori_loop(0, toks, count, (jnp.int32(0), jnp.int32(0)))
    several = jnp.int32(sets - 1)
    if sets > 2:
        several = jnp.where(total == 1, where - NEAR, several)
    case[0] = jnp.where(total == 0, 0, several)


def which_case(sets, spans, doc_start):
    return pl.pallas_call(
        functools.partial(case_kernel, sets),
        out_shape=jax.ShapeDtypeStruct((1,), jnp.int32),
        in_specs=[SMEM, SMEM],
        out_specs=SMEM,
        compiler_params=WHOLE,
        name="which_case",
    )(spans, doc_start)


def columns(head):
    return pl.ds(pl.multiple_of(head * HEAD_DIM, HEAD_DIM), HEAD_DIM)


def joined(blocks, which, part):
    return jnp.concatenate(
        [
            block[share, which, :, columns(part)]
            for block in blocks
            for share in range(block.shape[0])
        ],
        axis=0,
    )


def block_terms(part, allowed, blocks, data, store):
    queries, outgrads, norm, dot = data
    head_scale = 1.0 / math.sqrt(HEAD_DIM)
    heads = queries.shape[1] // QBLOCK
    allowed = jnp.concatenate([allowed] * heads, axis=1)
    keys, values = (joined(blocks, which, part) for which in range(2))
    scores = matmul(keys, queries[part], NT) * head_scale
    probs = jnp.where(allowed, jnp.exp(scores - norm[part]), 0.0)
    value_term = matmul(probs.astype(jnp.bfloat16), outgrads[part], NN)
    prob_grad = matmul(values, outgrads[part], NT)
    score_grad = (probs * (prob_grad - dot[part])).astype(jnp.bfloat16)
    key_term = matmul(score_grad, queries[part], NN)
    store(key_term * head_scale, value_term, score_grad)


def stage_kernel(
    spans, query, outgrad, norm, dot, starts_rows, queries, outgrads, norms, dots, lower
):
    tok = lax.axis_index("tok")
    parts, rows = queries.shape[:2]
    group = rows // QBLOCK
    for part in range(parts):
        for member in range(group):
            head = part * group + member
            place = slice(member * QBLOCK, (member + 1) * QBLOCK)
            queries[part, place, :] = query[:, head * HEAD_DIM : (head + 1) * HEAD_DIM]
            outgrads[part, place, :] = outgrad[:, head * HEAD_DIM : (head + 1) * HEAD_DIM]
            norms[part, :, place] = norm[head : head + 1, :]
            dots[part, :, place] = dot[head : head + 1, :]
    lower[...] = jnp.maximum(starts_rows[pl.ds(tok, 1), :], (tok - spans[tok] + 1) * QBLOCK)


def own_kernel(queries, outgrads, norms, dots, lower, block, own_terms, score_grads):
    tok = lax.axis_index("tok")
    key_row = lax.broadcasted_iota(jnp.int32, (QBLOCK, QBLOCK), 0)
    query_col = lax.broadcasted_iota(jnp.int32, (QBLOCK, QBLOCK), 1)
    allowed = (key_row + tok * QBLOCK >= lower[...]) & (key_row <= query_col)

    @pl.loop(0, score_grads.shape[0])
    def _(part):
        def store(key_term, value_term, score_grad):
            own_terms[0, :, columns(part)] = key_term
            own_terms[1, :, columns(part)] = value_term
            score_grads[part] = score_grad

        block_terms(part, allowed, [block], (queries, outgrads, norms, dots), store)


def more_kernel(first, *refs):
    data, lower, blocks = refs[:4], refs[4], refs[5:-2]
    terms, score_grads = refs[-2:]
    count = len(blocks)
    end = (lax.axis_index("tok") - first + 1) * QBLOCK
    read = jnp.min(lower[...]) < end

    @pl.when(jnp.logical_not(read))
    def _():
        terms[...] = jnp.zeros(terms.shape, terms.dtype)
        score_grads[...] = jnp.zeros(score_grads.shape, score_grads.dtype)

    @pl.when(read)
    def _():
        shape = (count * QBLOCK, QBLOCK)
        key_row = lax.broadcasted_iota(jnp.int32, shape, 0)
        allowed = key_row + (end - count * QBLOCK) >= lower[...]

        @pl.loop(0, score_grads.shape[0])
        def _(part):
            def store(key_term, value_term, score_grad):
                for slot in range(count):
                    rows = slice((count - 1 - slot) * QBLOCK, (count - slot) * QBLOCK)
                    terms[slot, 0, :, columns(part)] = key_term[rows].astype(terms.dtype)
                    terms[slot, 1, :, columns(part)] = value_term[rows].astype(terms.dtype)
                score_grads[part] = score_grad

            block_terms(part, allowed, blocks[::-1], data, store)


def query_kernel(counts, *refs):
    score_grads, blocks, query_grad = refs[: len(counts)], refs[len(counts) : -1], refs[-1]
    parts = score_grads[0].shape[0]
    group = score_grads[0].shape[2] // QBLOCK
    head_scale = 1.0 / math.sqrt(HEAD_DIM)
    in_order = []
    for count in counts:
        in_order += blocks[len(in_order) : len(in_order) + count][::-1]
    @pl.loop(0, parts)
    def _(part):
        keys = joined(in_order, 0, part)
        grads = jnp.concatenate([ref[part] for ref in score_grads], axis=0)
        total = (matmul(keys.T, grads, NN) * head_scale).astype(query_grad.dtype)
        for member in range(group):
            place = columns(part * group + member)
            query_grad[:, place] = total[:, member * QBLOCK : (member + 1) * QBLOCK].T


def sum_kernel(own, *refs):
    arrived, outs = refs[:-2], refs[-2:]
    for which, out in enumerate(outs):
        total = own[which]
        for term in arrived:
            total = total + term[which].astype(jnp.float32)
        out[...] = total.astype(out.dtype)


def cost(items, columns_here):
    return pl.CostEstimate(
        flops=items * 10 * QBLOCK * QBLOCK * columns_here,
        bytes_accessed=4 * 1024 * 1024,
        transcendentals=items * QBLOCK * columns_here,
    )


def per_device(query, keys, values, out_grad, log_norm, row_dot, doc_start, spans):
    toks, heads = lax.axis_size("tok"), lax.axis_size("head")
    key_cols = keys.shape[1] // heads
    parts = key_cols // HEAD_DIM
    rows = query.shape[1] // parts
    terms = (2, QBLOCK, key_cols)
    f32, bf16 = jnp.float32, jnp.bfloat16
    starts_rows = doc_start.reshape(-1, QBLOCK)
    sets = far_sets(toks)
    shares = pack(keys, values, heads)
    shares, spans_after = lax.optimization_barrier((shares, spans))
    case = which_case(len(sets), spans_after, doc_start)
    own = lax.all_to_all(shares, "head", split_axis=0, concat_axis=0)

    data = pl.pallas_call(
        stage_kernel,
        out_shape=(
            jax.ShapeDtypeStruct((parts, rows, HEAD_DIM), bf16),
            jax.ShapeDtypeStruct((parts, rows, HEAD_DIM), bf16),
            jax.ShapeDtypeStruct((parts, 1, rows), f32),
            jax.ShapeDtypeStruct((parts, 1, rows), f32),
            jax.ShapeDtypeStruct((1, QBLOCK), jnp.int32),
        ),
        in_specs=[SMEM] + [VMEM] * 5,
        out_specs=(VMEM,) * 5,
        compiler_params=STAGE,
        name="stage_queries",
    )(spans_after, query, out_grad, log_norm, row_dot, starts_rows)

    def own_part(data, own):
        return pl.pallas_call(
            own_kernel,
            out_shape=(
                jax.ShapeDtypeStruct(terms, f32),
                jax.ShapeDtypeStruct((parts, QBLOCK, rows), bf16),
            ),
            in_specs=[VMEM] * 6,
            out_specs=(VMEM,) * 2,
            compiler_params=LARGE,
            cost_estimate=cost(1, query.shape[1]),
            name="own_grads",
        )(*data, own)

    def more_part(first, data, blocks):
        return pl.pallas_call(
            functools.partial(more_kernel, first),
            out_shape=(
                jax.ShapeDtypeStruct((len(blocks), *terms), bf16),
                jax.ShapeDtypeStruct((parts, len(blocks) * QBLOCK, rows), bf16),
            ),
            in_specs=[VMEM] * (5 + len(blocks)),
            out_specs=(VMEM,) * 2,
            compiler_params=LARGE,
            cost_estimate=cost(len(blocks), query.shape[1]),
            name=f"grads_from_{first}",
        )(*data, *blocks)

    def branch(far_targets):
        far_steps = [steps for steps in range(NEAR + 1, REACH + 1) if far_targets]

        def targets_of(steps):
            return [target for target in far_targets if target >= steps]

        def run(data, own):
            near = [shifted(own, steps) for steps in range(1, NEAR + 1)]
            far = [
                shifted(own, steps, targets_of(steps)) if targets_of(steps) else own
                for steps in far_steps
            ]
            own_terms, own_grads = own_part(data, own)
            near_terms, near_grads = more_part(1, data, near)
            grads, blocks = [own_grads, near_grads], [[own], near]
            back = []
            for steps, arrived in zip(far_steps, far):
                targets = [target - steps for target in targets_of(steps)]
                if targets:
                    far_terms, far_grads = more_part(steps, data, [arrived])
                    grads.append(far_grads)
                    blocks.append([arrived])
                    back.append(shifted(far_terms[0], -steps, targets))
                    near_terms, _ = lax.optimization_barrier((near_terms, far_terms))
            back += [shifted(near_terms[steps - 1], -steps) for steps in range(1, NEAR + 1)]
            return finish(own_terms, back, grads, blocks)

        return run

    def finish(own_terms, back, grads, blocks):
        flat = [block for some in blocks for block in some]
        query_grad = pl.pallas_call(
            functools.partial(query_kernel, [len(some) for some in blocks]),
            out_shape=jax.ShapeDtypeStruct(query.shape, bf16),
            in_specs=[VMEM] * (len(grads) + len(flat)),
            out_specs=VMEM,
            compiler_params=LARGE,
            cost_estimate=pl.CostEstimate(
                flops=len(flat) * 2 * QBLOCK * query.size,
                bytes_accessed=query.size * 6,
                transcendentals=0,
            ),
            name="query_grad",
        )(*grads, *flat)
        key_grad, value_grad = pl.pallas_call(
            sum_kernel,
            out_shape=(jax.ShapeDtypeStruct(terms[1:], bf16),) * 2,
            in_specs=[VMEM] * (1 + len(back)),
            out_specs=(VMEM,) * 2,
            compiler_params=SMALL,
            name="sum_terms",
        )(own_terms, *back)
        return query_grad, key_grad, value_grad

    return lax.switch(case[0], [branch(targets) for targets in sets], data, own)


def solution(mesh):
    in_specs = (
        P("tok", "head"),
        P(("tok", "head"), None),
        P(("tok", "head"), None),
        P("tok", "head"),
        P("head", "tok"),
        P("head", "tok"),
        P(),
        P(),
    )
    out_specs = (P("tok", "head"), P("tok", "head"), P("tok", "head"))
    return jax.shard_map(
        per_device, mesh=mesh, in_specs=in_specs, out_specs=out_specs, check_vma=False
    )
```

```python
import functools
import math

import jax
import jax.numpy as jnp
from jax import lax
from jax.experimental import pallas as pl
from jax.experimental.pallas import tpu as pltpu
from jax.sharding import PartitionSpec as P

HEADS = 64
KV_HEADS = 8
HEAD_DIM = 128
QBLOCK = 128
REACH = 5
NEAR = 2
ABLE_MAX = 5
NT = (((1,), (1,)), ((), ()))
NN = (((1,), (0,)), ((), ()))
HBM = pl.BlockSpec(memory_space=pltpu.HBM)
VMEM = pl.BlockSpec(memory_space=pltpu.VMEM)
SMEM = pl.BlockSpec(memory_space=pltpu.SMEM)
WHOLE = pltpu.CompilerParams(vmem_limit_bytes=60 * 1024 * 1024)
STAGE = pltpu.CompilerParams(vmem_limit_bytes=56 * 1024 * 1024)
LARGE = pltpu.CompilerParams(vmem_limit_bytes=24 * 1024 * 1024)
SMALL = pltpu.CompilerParams(vmem_limit_bytes=6 * 1024 * 1024)


def matmul(left, right, dims):
    return lax.dot_general(left, right, dims, preferred_element_type=jnp.float32)


def shifted(value, steps, targets=None):
    count = lax.axis_size("tok")
    if targets is None:
        targets = range(max(0, steps), min(count, count + steps))
    return lax.ppermute(value, "tok", [(target - steps, target) for target in targets])


def far_sets(toks):
    able = list(range(NEAR + 1, toks))
    return [[], *([tok] for tok in able if len(able) <= ABLE_MAX), able]


def blocks_read(tok, spans, starts):
    lowest = starts[tok * QBLOCK] // QBLOCK
    return jnp.minimum(spans[tok], tok - lowest + 1)


def pack_kernel(keys, values, shares, held, packed, came, left):
    heads, key_cols = shares.shape[0], shares.shape[-1]
    arrivals = [
        pltpu.make_async_copy(source, held.at[which], came.at[which])
        for which, source in enumerate((keys, values))
    ]
    departures = [
        [
            pltpu.make_async_copy(
                packed.at[which, head], shares.at[head, which], left.at[which, head]
            )
            for head in range(heads)
        ]
        for which in range(2)
    ]
    for arrival in arrivals:
        arrival.start()
    for which in range(2):
        arrivals[which].wait()
        for head in range(heads):
            packed[which, head] = held[which, :, head * key_cols : (head + 1) * key_cols]
            departures[which][head].start()
    for departure in departures[0] + departures[1]:
        departure.wait()


def pack(keys, values, heads):
    rows, key_cols = keys.shape[0], keys.shape[1] // heads
    return pl.pallas_call(
        pack_kernel,
        out_shape=jax.ShapeDtypeStruct((heads, 2, rows, key_cols), keys.dtype),
        in_specs=[HBM, HBM],
        out_specs=HBM,
        scratch_shapes=[
            pltpu.VMEM((2, *keys.shape), keys.dtype),
            pltpu.VMEM((2, heads, rows, key_cols), keys.dtype),
            pltpu.SemaphoreType.DMA((2,)),
            pltpu.SemaphoreType.DMA((2, heads)),
        ],
        compiler_params=WHOLE,
        name="pack_shares",
    )(keys, values)


def case_kernel(sets, spans, starts, case):
    toks = spans.shape[0]

    def far(tok):
        return blocks_read(tok, spans, starts) > NEAR + 1

    def count(tok, seen):
        read = far(tok).astype(jnp.int32)
        return seen[0] + read, seen[1] + read * tok

    total, where = lax.fori_loop(0, toks, count, (jnp.int32(0), jnp.int32(0)))
    several = jnp.int32(sets - 1)
    if sets > 2:
        several = jnp.where(total == 1, where - NEAR, several)
    case[0] = jnp.where(total == 0, 0, several)


def which_case(sets, spans, doc_start):
    return pl.pallas_call(
        functools.partial(case_kernel, sets),
        out_shape=jax.ShapeDtypeStruct((1,), jnp.int32),
        in_specs=[SMEM, SMEM],
        out_specs=SMEM,
        compiler_params=WHOLE,
        name="which_case",
    )(spans, doc_start)


def columns(head):
    return pl.ds(pl.multiple_of(head * HEAD_DIM, HEAD_DIM), HEAD_DIM)


def joined(blocks, which, part):
    return jnp.concatenate(
        [
            block[share, which, :, columns(part)]
            for block in blocks
            for share in range(block.shape[0])
        ],
        axis=0,
    )


def block_terms(part, allowed, blocks, data, store):
    queries, outgrads, norm, dot = data
    head_scale = 1.0 / math.sqrt(HEAD_DIM)
    heads = queries.shape[1] // QBLOCK
    allowed = jnp.concatenate([allowed] * heads, axis=1)
    keys, values = (joined(blocks, which, part) for which in range(2))
    scores = matmul(keys, queries[part], NT) * head_scale
    probs = jnp.where(allowed, jnp.exp(scores - norm[part]), 0.0)
    value_term = matmul(probs.astype(jnp.bfloat16), outgrads[part], NN)
    prob_grad = matmul(values, outgrads[part], NT)
    score_grad = (probs * (prob_grad - dot[part])).astype(jnp.bfloat16)
    key_term = matmul(score_grad, queries[part], NN)
    store(key_term * head_scale, value_term, score_grad)


def stage_kernel(
    spans, query, outgrad, norm, dot, starts_rows, queries, outgrads, norms, dots, lower
):
    tok = lax.axis_index("tok")
    parts, rows = queries.shape[:2]
    group = rows // QBLOCK
    for part in range(parts):
        for member in range(group):
            head = part * group + member
            place = slice(member * QBLOCK, (member + 1) * QBLOCK)
            queries[part, place, :] = query[:, head * HEAD_DIM : (head + 1) * HEAD_DIM]
            outgrads[part, place, :] = outgrad[:, head * HEAD_DIM : (head + 1) * HEAD_DIM]
            norms[part, :, place] = norm[head : head + 1, :]
            dots[part, :, place] = dot[head : head + 1, :]
    lower[...] = jnp.maximum(starts_rows[pl.ds(tok, 1), :], (tok - spans[tok] + 1) * QBLOCK)


def own_kernel(queries, outgrads, norms, dots, lower, block, own_terms, score_grads):
    tok = lax.axis_index("tok")
    key_row = lax.broadcasted_iota(jnp.int32, (QBLOCK, QBLOCK), 0)
    query_col = lax.broadcasted_iota(jnp.int32, (QBLOCK, QBLOCK), 1)
    allowed = (key_row + tok * QBLOCK >= lower[...]) & (key_row <= query_col)

    @pl.loop(0, score_grads.shape[0])
    def _(part):
        def store(key_term, value_term, score_grad):
            own_terms[0, :, columns(part)] = key_term
            own_terms[1, :, columns(part)] = value_term
            score_grads[part] = score_grad

        block_terms(part, allowed, [block], (queries, outgrads, norms, dots), store)


def more_kernel(first, *refs):
    data, lower, blocks = refs[:4], refs[4], refs[5:-2]
    terms, score_grads = refs[-2:]
    count = len(blocks)
    end = (lax.axis_index("tok") - first + 1) * QBLOCK
    read = jnp.min(lower[...]) < end

    @pl.when(jnp.logical_not(read))
    def _():
        terms[...] = jnp.zeros(terms.shape, terms.dtype)
        score_grads[...] = jnp.zeros(score_grads.shape, score_grads.dtype)

    @pl.when(read)
    def _():
        shape = (count * QBLOCK, QBLOCK)
        key_row = lax.broadcasted_iota(jnp.int32, shape, 0)
        allowed = key_row + (end - count * QBLOCK) >= lower[...]

        @pl.loop(0, score_grads.shape[0])
        def _(part):
            def store(key_term, value_term, score_grad):
                for slot in range(count):
                    rows = slice((count - 1 - slot) * QBLOCK, (count - slot) * QBLOCK)
                    terms[slot, 0, :, columns(part)] = key_term[rows].astype(terms.dtype)
                    terms[slot, 1, :, columns(part)] = value_term[rows].astype(terms.dtype)
                score_grads[part] = score_grad

            block_terms(part, allowed, blocks[::-1], data, store)


def query_kernel(counts, *refs):
    score_grads, blocks, query_grad = refs[: len(counts)], refs[len(counts) : -1], refs[-1]
    parts = score_grads[0].shape[0]
    group = score_grads[0].shape[2] // QBLOCK
    head_scale = 1.0 / math.sqrt(HEAD_DIM)
    in_order = []
    for count in counts:
        in_order += blocks[len(in_order) : len(in_order) + count][::-1]
    @pl.loop(0, parts)
    def _(part):
        keys = joined(in_order, 0, part)
        grads = jnp.concatenate([ref[part] for ref in score_grads], axis=0)
        total = (matmul(keys.T, grads, NN) * head_scale).astype(query_grad.dtype)
        for member in range(group):
            place = columns(part * group + member)
            query_grad[:, place] = total[:, member * QBLOCK : (member + 1) * QBLOCK].T


def sum_kernel(own, *refs):
    arrived, outs = refs[:-2], refs[-2:]
    for which, out in enumerate(outs):
        total = own[which]
        for term in arrived:
            total = total + term[which].astype(jnp.float32)
        out[...] = total.astype(out.dtype)


def cost(items, columns_here):
    return pl.CostEstimate(
        flops=items * 10 * QBLOCK * QBLOCK * columns_here,
        bytes_accessed=4 * 1024 * 1024,
        transcendentals=items * QBLOCK * columns_here,
    )


def per_device(query, keys, values, out_grad, log_norm, row_dot, doc_start, spans):
    toks, heads = lax.axis_size("tok"), lax.axis_size("head")
    key_cols = keys.shape[1] // heads
    parts = key_cols // HEAD_DIM
    rows = query.shape[1] // parts
    terms = (2, QBLOCK, key_cols)
    f32, bf16 = jnp.float32, jnp.bfloat16
    starts_rows = doc_start.reshape(-1, QBLOCK)
    sets = far_sets(toks)
    shares = pack(keys, values, heads)
    shares, spans_after = lax.optimization_barrier((shares, spans))
    case = which_case(len(sets), spans_after, doc_start)
    own = lax.all_to_all(shares, "head", split_axis=0, concat_axis=0)

    data = pl.pallas_call(
        stage_kernel,
        out_shape=(
            jax.ShapeDtypeStruct((parts, rows, HEAD_DIM), bf16),
            jax.ShapeDtypeStruct((parts, rows, HEAD_DIM), bf16),
            jax.ShapeDtypeStruct((parts, 1, rows), f32),
            jax.ShapeDtypeStruct((parts, 1, rows), f32),
            jax.ShapeDtypeStruct((1, QBLOCK), jnp.int32),
        ),
        in_specs=[SMEM] + [VMEM] * 5,
        out_specs=(VMEM,) * 5,
        compiler_params=STAGE,
        name="stage_queries",
    )(spans_after, query, out_grad, log_norm, row_dot, starts_rows)

    def own_part(data, own):
        return pl.pallas_call(
            own_kernel,
            out_shape=(
                jax.ShapeDtypeStruct(terms, f32),
                jax.ShapeDtypeStruct((parts, QBLOCK, rows), bf16),
            ),
            in_specs=[VMEM] * 6,
            out_specs=(VMEM,) * 2,
            compiler_params=LARGE,
            cost_estimate=cost(1, query.shape[1]),
            name="own_grads",
        )(*data, own)

    def more_part(first, data, blocks):
        return pl.pallas_call(
            functools.partial(more_kernel, first),
            out_shape=(
                jax.ShapeDtypeStruct((len(blocks), *terms), bf16),
                jax.ShapeDtypeStruct((parts, len(blocks) * QBLOCK, rows), bf16),
            ),
            in_specs=[VMEM] * (5 + len(blocks)),
            out_specs=(VMEM,) * 2,
            compiler_params=LARGE,
            cost_estimate=cost(len(blocks), query.shape[1]),
            name=f"grads_from_{first}",
        )(*data, *blocks)

    def branch(far_targets):
        far_steps = [steps for steps in range(NEAR + 1, REACH + 1) if far_targets]

        def targets_of(steps):
            return [target for target in far_targets if target >= steps]

        def run(data, own):
            near = [shifted(own, steps) for steps in range(1, NEAR + 1)]
            far = [
                shifted(own, steps, targets_of(steps)) if targets_of(steps) else own
                for steps in far_steps
            ]
            own_terms, own_grads = own_part(data, own)
            near_terms, near_grads = more_part(1, data, near)
            grads, blocks = [own_grads, near_grads], [[own], near]
            back = []
            for steps, arrived in zip(far_steps, far):
                targets = [target - steps for target in targets_of(steps)]
                if targets:
                    far_terms, far_grads = more_part(steps, data, [arrived])
                    grads.append(far_grads)
                    blocks.append([arrived])
                    back.append(shifted(far_terms[0], -steps, targets))
                    near_terms, _ = lax.optimization_barrier((near_terms, far_terms))
            back += [shifted(near_terms[steps - 1], -steps) for steps in range(1, NEAR + 1)]
            return finish(own_terms, back, grads, blocks)

        return run

    def finish(own_terms, back, grads, blocks):
        flat = [block for some in blocks for block in some]
        query_grad = pl.pallas_call(
            functools.partial(query_kernel, [len(some) for some in blocks]),
            out_shape=jax.ShapeDtypeStruct(query.shape, bf16),
            in_specs=[VMEM] * (len(grads) + len(flat)),
            out_specs=VMEM,
            compiler_params=LARGE,
            cost_estimate=pl.CostEstimate(
                flops=len(flat) * 2 * QBLOCK * query.size,
                bytes_accessed=query.size * 6,
                transcendentals=0,
            ),
            name="query_grad",
        )(*grads, *flat)
        key_grad, value_grad = pl.pallas_call(
            sum_kernel,
            out_shape=(jax.ShapeDtypeStruct(terms[1:], bf16),) * 2,
            in_specs=[VMEM] * (1 + len(back)),
            out_specs=(VMEM,) * 2,
            compiler_params=SMALL,
            name="sum_terms",
        )(own_terms, *back)
        return query_grad, key_grad, value_grad

    return lax.switch(case[0], [branch(targets) for targets in sets], data, own)


def solution(mesh):
    in_specs = (
        P("tok", "head"),
        P(("tok", "head"), None),
        P(("tok", "head"), None),
        P("tok", "head"),
        P("head", "tok"),
        P("head", "tok"),
        P(),
        P(),
    )
    out_specs = (P("tok", "head"), P("tok", "head"), P("tok", "head"))
    return jax.shard_map(
        per_device, mesh=mesh, in_specs=in_specs, out_specs=out_specs, check_vma=False
    )
```
